256 devices in a mesh: gx: 32 (over y, z_lo, x), gy: 8 (over z_hi, core).
Axes of the slice: x: 4, y: 4, z: 8 (z_hi: 4, z_lo: 2; z = z_hi * 2 + z_lo), core: 2. Of those that a mesh axis runs over, the one named last changes fastest.
Arguments:
- node_latents: bfloat16 [32, 8, 256, 512], P('gx', 'gy'), may hold values from -6 to 6
- edge_latents: bfloat16 [32, 8, 768, 512], P('gx', 'gy'), may hold values from -6 to 6
- edge_w1: bfloat16 [1536, 512], replicated, may hold values from -0.15625 to 0.15625
- edge_b1: float32 [512], replicated, may hold values from -3 to 3
- edge_w2: bfloat16 [512, 512], replicated, may hold values from -0.25 to 0.25
- node_w1: bfloat16 [1024, 512], replicated, may hold values from -0.1875 to 0.1875
- node_b1: float32 [512], replicated, may hold values from -3 to 3
- node_w2: bfloat16 [512, 512], replicated, may hold values from -0.25 to 0.25
- node_cot: bfloat16 [32, 8, 256, 512], P('gx', 'gy'), may hold values from -6 to 6
- edge_cot: bfloat16 [32, 8, 768, 512], P('gx', 'gy'), may hold values from -6 to 6
- send_count: int32 [32, 8, 4], P('gx', 'gy'), may hold values from 0 to 2, as said below
- send_list: int32 [32, 8, 4, 2], P('gx', 'gy'), may hold values from 0 to 1
- tile_recv: int32 [32, 8, 6], P('gx', 'gy'), may hold values from 0 to 1
- tile_send: int32 [32, 8, 6], P('gx', 'gy'), may hold values from 0 to 9, as said below
- tile_perm: int32 [32, 8, 6, 128], P('gx', 'gy'), may hold values from 0 to 127, each once within a row
Outputs:
- node_out: bfloat16 [32, 8, 256, 512], P('gx', 'gy')
- node_grad: bfloat16 [32, 8, 256, 512], P('gx', 'gy')
- edge_grad: bfloat16 [32, 8, 768, 512], P('gx', 'gy')
- weight_dir: bfloat16 [1835008], P(('gx', 'gy'))
The draws below stay inside these ranges and needn't reach their ends.
Inputs may be any that keep to these rules, and one draw needn't show every extreme that they name: `send_count`: entries for a neighbour outside the grid of partitions are 0, all others at least 1; the partition at (0, 0) sends 2 blocks to its neighbour at gx+1. `tile_send`: A value of 2 or more is a halo slot 2 + d * 2 + s that direction d's neighbour fills (s below its send count).
All inputs are finite; a program needn't handle non-finite values.
Results may differ from the reference program's by a relative error of at most 0.0075.
Values may be sent and summed in bfloat16 or wider, within the bound.
A program may use at most 128 MiB of HBM per device.

```python
import jax
import jax.numpy as jnp
from jax import lax

D = 512
BLOCK = 128
NB = 2
MAXB = 2
NODES_DEV = 256
TILES = 6
EDGES_DEV = 768
NBX = 10
N_GX = 32
N_GY = 8


def halo_counts(key):
    counts = jax.random.randint(jax.random.fold_in(key, 11), (N_GX, N_GY, 4), 1, MAXB + 1)
    row_ids = jnp.arange(N_GX)[:, None, None]
    col_ids = jnp.arange(N_GY)[None, :, None]
    direction = jnp.arange(4)[None, None, :]
    exists = (direction == 0) & (row_ids < N_GX - 1) | (direction == 1) & (row_ids > 0) | (direction == 2) & (col_ids < N_GY - 1) | (direction == 3) & (col_ids > 0)
    counts = jnp.where(exists, counts, 0)
    counts = counts.at[0, 0, 0].set(MAXB)
    return counts.astype(jnp.int32)


def draw_send_count(key, part):
    return halo_counts(key)


def draw_tile_send(key, part):
    counts = halo_counts(key)
    zero_row = jnp.zeros((1, N_GY), jnp.int32)
    zero_col = jnp.zeros((N_GX, 1), jnp.int32)
    recv_zero = jnp.concatenate([zero_row, counts[:-1, :, 0]], axis=0)
    recv_one = jnp.concatenate([counts[1:, :, 1], zero_row], axis=0)
    recv_two = jnp.concatenate([zero_col, counts[:, :-1, 2]], axis=1)
    recv_three = jnp.concatenate([counts[:, 1:, 3], zero_col], axis=1)
    recv_counts = jnp.stack([recv_zero, recv_one, recv_two, recv_three], axis=2)
    shape = (N_GX, N_GY, TILES)
    local_pick = jax.random.randint(jax.random.fold_in(key, 21), shape, 0, NB)
    direction = jax.random.randint(jax.random.fold_in(key, 22), shape, 0, 4)
    coin_flip = jax.random.randint(jax.random.fold_in(key, 23), shape, 0, 2)
    available = jnp.take_along_axis(recv_counts, direction, axis=2)
    slot_pick = jax.random.randint(jax.random.fold_in(key, 24), shape, 0, MAXB) % jnp.maximum(available, 1)
    halo_block = NB + direction * MAXB + slot_pick
    chosen = (coin_flip == 1) & (available > 0)
    return jnp.where(chosen, halo_block, local_pick).astype(jnp.int32)


def with_ends(array, rng, smallest, high):
    longest = array.shape.index(max(array.shape))
    spots = []
    for shift in (0, 1):
        where = [jax.random.randint(jax.random.fold_in(rng, axis), (), 0, length) for axis, length in enumerate(array.shape)]
        where[longest] = (where[longest] + shift) % array.shape[longest]
        spots.append(tuple(where))
    return array.at[spots[0]].set(smallest).at[spots[1]].set(high)


def level_of(own_key, shape, shards, low, largest):
    def one(axis_at, blocks):
        steps = jax.random.uniform(jax.random.fold_in(jax.random.fold_in(own_key, 6), axis_at), (blocks,), jnp.float32, low / len(shards), largest / len(shards))
        return jnp.repeat(jnp.exp(steps), shape[axis_at] // blocks).reshape((-1,) + (1,) * (len(shape) - axis_at - 1))

    level = one(*shards[0])
    for cut in shards[1:]:
        level = level * one(*cut)
    return level


def centred(stream_key, shape, width, reach, split=(), kind=jnp.bfloat16):
    array = width * jax.random.normal(stream_key, shape, jnp.float32)
    if split:
        array = array * level_of(stream_key, shape, split, -0.22, 0.18)
    return jnp.clip(array, -reach, reach).astype(kind)


def setup_inputs(seed: int = 0) -> dict:
    key_of = jax.random.split(jax.random.key(seed), 16)
    node_latents = centred(key_of[0], (N_GX, N_GY, NODES_DEV, D), 1.0, 6.0, ((0, 32), (1, 8)))
    edge_latents = centred(key_of[1], (N_GX, N_GY, EDGES_DEV, D), 1.0, 6.0, ((0, 32), (1, 8)))
    edge_w1 = centred(key_of[2], (3 * D, D), (3 * D) ** -0.5, 0.15625)
    edge_b1 = centred(key_of[3], (D,), 0.5, 3.0, (), jnp.float32)
    edge_w2 = centred(key_of[4], (D, D), D ** -0.5, 0.25)
    node_w1 = centred(key_of[5], (2 * D, D), (2 * D) ** -0.5, 0.1875)
    node_b1 = centred(key_of[6], (D,), 0.5, 3.0, (), jnp.float32)
    node_w2 = centred(key_of[7], (D, D), D ** -0.5, 0.25)
    node_cot = centred(key_of[8], (N_GX, N_GY, NODES_DEV, D), 1.0, 6.0, ((0, 32), (1, 8)))
    edge_cot = centred(key_of[9], (N_GX, N_GY, EDGES_DEV, D), 1.0, 6.0, ((0, 32), (1, 8)))
    send_count = draw_send_count(jax.random.fold_in(key_of[15], 71), 0)
    send_list = with_ends(jax.random.randint(key_of[11], (N_GX, N_GY, 4, MAXB), 0, NB), jax.random.fold_in(key_of[11], 1), 0, NB - 1).astype(jnp.int32)
    tile_recv = with_ends(jax.random.randint(key_of[12], (N_GX, N_GY, TILES), 0, NB), jax.random.fold_in(key_of[12], 1), 0, NB - 1).astype(jnp.int32)
    tile_send = draw_tile_send(jax.random.fold_in(key_of[15], 71), 0)
    tile_perm = jax.vmap(lambda own: jax.random.permutation(own, BLOCK))(jax.random.split(key_of[14], N_GX * N_GY * TILES)).reshape((N_GX, N_GY, TILES, BLOCK)).astype(jnp.int32)
    return dict(node_latents=node_latents, edge_latents=edge_latents, edge_w1=edge_w1, edge_b1=edge_b1, edge_w2=edge_w2, node_w1=node_w1, node_b1=node_b1, node_w2=node_w2, node_cot=node_cot, edge_cot=edge_cot, send_count=send_count, send_list=send_list, tile_recv=tile_recv, tile_send=tile_send, tile_perm=tile_perm)


def silu_slope(values):
    logistic = jax.nn.sigmoid(values)
    return logistic * (1.0 + values * (1.0 - logistic))

def layer_norm(values):
    center = values - lax.optimization_barrier(jnp.mean(values, axis=-1, keepdims=True))
    inverse_rms = lax.rsqrt(lax.optimization_barrier(jnp.mean(center * center, axis=-1, keepdims=True)) + 1e-05)
    return (center * inverse_rms, inverse_rms)

def norm_back(normed, inverse_rms, upstream):
    return inverse_rms * (upstream - lax.optimization_barrier(jnp.mean(upstream, axis=-1, keepdims=True)) - normed * lax.optimization_barrier(jnp.mean(upstream * normed, axis=-1, keepdims=True)))

def from_lower(values, axis):
    leading = jnp.zeros_like(lax.slice_in_dim(values, 0, 1, axis=axis))
    return jnp.concatenate([leading, lax.slice_in_dim(values, 0, values.shape[axis] - 1, axis=axis)], axis=axis)

def from_upper(values, axis):
    trailing = jnp.zeros_like(lax.slice_in_dim(values, 0, 1, axis=axis))
    return jnp.concatenate([lax.slice_in_dim(values, 1, values.shape[axis], axis=axis), trailing], axis=axis)

def local_pass(extended, edge_rows, cot_node, cot_edge, recv_idx, send_idx, perm_idx, weights):
    edge_w1, edge_b1, edge_w2, node_w1, node_b1, node_w2 = weights
    flat_ext = extended.reshape(NBX * BLOCK, D)
    local_rows = extended[:NB].reshape(NB * BLOCK, D)
    offsets = jnp.arange(BLOCK, dtype=jnp.int32)
    recv_rows = (recv_idx[:, None] * BLOCK + offsets[None, :]).reshape(-1)
    send_rows = (send_idx[:, None] * BLOCK + perm_idx).reshape(-1)
    h_recv = flat_ext[recv_rows]
    h_send = flat_ext[send_rows]
    joined = jnp.concatenate([edge_rows, h_recv, h_send], axis=1)
    edge_affine = jnp.dot(joined, edge_w1, preferred_element_type=jnp.float32) + edge_b1
    edge_hidden = jax.nn.silu(edge_affine).astype(jnp.bfloat16)
    edge_linear = jnp.dot(edge_hidden, edge_w2, preferred_element_type=jnp.float32)
    message, edge_inv = layer_norm(edge_linear)
    recv_hot = (recv_idx[None, :] == jnp.arange(NB, dtype=jnp.int32)[:, None]).astype(jnp.float32)
    aggregate = jnp.einsum('bt,tnf->bnf', recv_hot, message.reshape(TILES, BLOCK, D), precision=lax.Precision.HIGHEST)
    aggregate = aggregate.reshape(NB * BLOCK, D).astype(jnp.bfloat16)
    node_input = jnp.concatenate([local_rows, aggregate], axis=1)
    node_affine = jnp.dot(node_input, node_w1, preferred_element_type=jnp.float32) + node_b1
    node_hidden = jax.nn.silu(node_affine).astype(jnp.bfloat16)
    node_linear = jnp.dot(node_hidden, node_w2, preferred_element_type=jnp.float32)
    node_normed, node_inv = layer_norm(node_linear)
    node_out = (local_rows.astype(jnp.float32) + node_normed).astype(jnp.bfloat16)
    grad_node_linear = norm_back(node_normed, node_inv, cot_node.astype(jnp.float32)).astype(jnp.bfloat16)
    g_nw2 = jnp.dot(node_hidden.T, grad_node_linear, preferred_element_type=jnp.float32)
    grad_node_affine = (jnp.dot(grad_node_linear, node_w2.T, preferred_element_type=jnp.float32) * silu_slope(node_affine)).astype(jnp.bfloat16)
    g_nw1 = jnp.dot(node_input.T, grad_node_affine, preferred_element_type=jnp.float32)
    grad_node_input = jnp.dot(grad_node_affine, node_w1.T, preferred_element_type=jnp.float32)
    grad_direct = grad_node_input[:, :D]
    grad_aggregate = grad_node_input[:, D:]
    grad_message = grad_aggregate[recv_rows] + cot_edge.astype(jnp.float32)
    grad_edge_linear = norm_back(message, edge_inv, grad_message).astype(jnp.bfloat16)
    g_ew2 = jnp.dot(edge_hidden.T, grad_edge_linear, preferred_element_type=jnp.float32)
    grad_edge_affine = (jnp.dot(grad_edge_linear, edge_w2.T, preferred_element_type=jnp.float32) * silu_slope(edge_affine)).astype(jnp.bfloat16)
    g_ew1 = jnp.dot(joined.T, grad_edge_affine, preferred_element_type=jnp.float32)
    grad_joined = jnp.dot(grad_edge_affine, edge_w1.T, preferred_element_type=jnp.float32)
    edge_grad = (cot_edge.astype(jnp.float32) + grad_joined[:, :D]).astype(jnp.bfloat16)
    grad_recv = jnp.einsum('bt,tnf->bnf', recv_hot, grad_joined[:, D:2 * D].reshape(TILES, BLOCK, D), precision=lax.Precision.HIGHEST)
    inverse = jnp.argsort(perm_idx, axis=1).astype(jnp.int32)
    grad_send = jnp.take_along_axis(grad_joined[:, 2 * D:].reshape(TILES, BLOCK, D), inverse[:, :, None], axis=1)
    send_hot = (send_idx[None, :] == jnp.arange(NBX, dtype=jnp.int32)[:, None]).astype(jnp.float32)
    partial_sum = jnp.einsum('bt,tnf->bnf', send_hot, grad_send, precision=lax.Precision.HIGHEST)
    owned_part = partial_sum[:NB] + grad_recv + grad_direct.reshape(NB, BLOCK, D)
    halo_part = partial_sum[NB:]
    weight_grad = jnp.concatenate([g_ew1, g_ew2, g_nw1, g_nw2], axis=0)
    return (node_out, edge_grad, owned_part, halo_part, weight_grad)

def rms_normalize(total):
    bounds = [0, 3 * D, 4 * D, 6 * D, 7 * D]
    pieces = []
    for index in range(4):
        matrix = total[bounds[index]:bounds[index + 1]]
        pieces.append(matrix * lax.rsqrt(jnp.mean(matrix * matrix) + 1e-06))
    return jnp.concatenate(pieces, axis=0).astype(jnp.bfloat16)

def reference(node_latents, edge_latents, edge_w1, edge_b1, edge_w2, node_w1, node_b1, node_w2, node_cot, edge_cot, send_count, send_list, tile_recv, tile_send, tile_perm):
    weights = (edge_w1, edge_b1, edge_w2, node_w1, node_b1, node_w2)
    node_blocks = node_latents.reshape(N_GX, N_GY, NB, BLOCK, D)
    flat_lists = send_list.reshape(N_GX, N_GY, 4 * MAXB)
    packed = jax.vmap(jax.vmap(lambda source, chosen: source[chosen]))(node_blocks, flat_lists)
    packed = packed.reshape(N_GX, N_GY, 4, MAXB, BLOCK, D)
    live_slots = jnp.arange(MAXB, dtype=jnp.int32)[None, None, None, :] < send_count[..., None]
    packed = jnp.where(live_slots[..., None, None], packed, jnp.zeros((), packed.dtype))
    halo_blocks = jnp.stack([from_lower(packed[:, :, 0], 0), from_upper(packed[:, :, 1], 0), from_lower(packed[:, :, 2], 1), from_upper(packed[:, :, 3], 1)], axis=2)
    halo_blocks = halo_blocks.reshape(N_GX, N_GY, 4 * MAXB, BLOCK, D)
    extended = jnp.concatenate([node_blocks, halo_blocks], axis=2)
    items = (extended.reshape(-1, NBX, BLOCK, D), edge_latents.reshape(-1, EDGES_DEV, D), node_cot.reshape(-1, NODES_DEV, D), edge_cot.reshape(-1, EDGES_DEV, D), tile_recv.reshape(-1, TILES), tile_send.reshape(-1, TILES), tile_perm.reshape(-1, TILES, BLOCK))

    def visit(total, item):
        result = local_pass(*item, weights)
        return (total + result[4], result[:4])
    total, (node_out, edge_grad, owned_part, halo_part) = lax.scan(visit, jnp.zeros((7 * D, D), jnp.float32), items)
    halo_part = halo_part.reshape(N_GX, N_GY, 4, MAXB, BLOCK, D)
    returned = jnp.stack([from_upper(halo_part[:, :, 0], 0), from_lower(halo_part[:, :, 1], 0), from_upper(halo_part[:, :, 2], 1), from_lower(halo_part[:, :, 3], 1)], axis=2)
    back_hot = ((send_list[..., None] == jnp.arange(NB, dtype=jnp.int32)) & live_slots[..., None]).astype(jnp.float32)
    contrib = jnp.einsum('xyqsb,xyqsnf->xybnf', back_hot, returned, precision=lax.Precision.HIGHEST)
    node_grad = node_cot.reshape(N_GX, N_GY, NB, BLOCK, D).astype(jnp.float32) + owned_part.reshape(N_GX, N_GY, NB, BLOCK, D) + contrib
    node_grad = node_grad.astype(jnp.bfloat16).reshape(N_GX, N_GY, NODES_DEV, D)
    weight_dir = rms_normalize(total).reshape(7 * D * D)
    return (node_out.reshape(N_GX, N_GY, NODES_DEV, D), node_grad, edge_grad.reshape(N_GX, N_GY, EDGES_DEV, D), weight_dir)
```

```python
import functools

import jax
import jax.numpy as jnp
from jax import lax
from jax.experimental import pallas as pl
from jax.experimental.pallas import tpu as pltpu
from jax.sharding import PartitionSpec as P

MESH = pl.DeviceIdType.MESH
F32 = jnp.float32
BF16 = jnp.bfloat16
D = 512
H = 256
Q = 128
ROWS = 7 * D
CHIP_ROWS = 28
BLK = 112
NGROUP = 8
EARLY = 5
BOUNDS = (3 * D, 4 * D, 6 * D)
SIZES = (3 * D * D, D * D, 2 * D * D, D * D)
PIECES = ((4 * D, 3 * D), (3 * D, D), (0, D), (D, D), (2 * D, D))


def dot(a, b):
    return jnp.dot(a, b, preferred_element_type=F32)


def dot_t(a, b):
    return lax.dot_general(a, b, (((1,), (1,)), ((), ())), preferred_element_type=F32)


def t_dot(a, b):
    return lax.dot_general(a, b, (((0,), (0,)), ((), ())), preferred_element_type=F32)


def normed_rows(values):
    center = values - jnp.mean(values, axis=-1, keepdims=True)
    inv = lax.rsqrt(jnp.mean(center * center, axis=-1, keepdims=True) + 1e-05)
    return center * inv, inv


def norm_back(normed, inv, up):
    return inv * (
        up
        - jnp.mean(up, axis=-1, keepdims=True)
        - normed * jnp.mean(up * normed, axis=-1, keepdims=True)
    )


def silu_parts(v):
    s = jax.nn.sigmoid(v)
    return (v * s).astype(BF16), s * (1.0 + v * (1.0 - s))


def picked(flag):
    return jnp.where(flag, 1.0, 0.0).astype(F32)


def kernel(
    count_s, list_s, recv_s, send_s, perm_ref, eb1, nb1,
    nodes_h, edges_h, ew1_h, ew2_h, nw1_h, nw2_h, cotn_h, cote_h,
    nout_h, ngrad_h, egrad_h, wdir,
    loc, ext, edges, ew1, ew2, nw1, nw2, cotn, cote, pack, pt, pm,
    hr, hs, aff, hid, msg, einv, agg, gagg, owned, gea, geap, gel_p,
    nin, gna_p, gnl_p, xs, hret, ret, nout, ngrad, egrad,
    gsend, gown, grecv, g1a, g1b, r1a, r1b, g2a, g2b, r2a, r2b,
    g3, s3, r3, fin, swap_s, swap_r, stat_s, stat_r, flat,
    in_sem, out_sem, hs_sem, hr_sem, bs_sem, br_sem, cs_sem, cr_sem,
    as_sem, ar_sem, ys_sem, yr_sem, a2s_sem, a2r_sem, b2s_sem, b2r_sem,
    zs_sem, zr_sem, ws_sem, wr_sem, ts_sem, tr_sem,
):
    gx = lax.axis_index("gx")
    gy = lax.axis_index("gy")
    y = gx // 8
    z_lo = (gx // 4) % 2
    x = gx % 4
    z_hi = gy // 2
    core = gy % 2
    z = z_hi * 2 + z_lo
    other = (gx, z_hi * 2 + (1 - core))

    def x_peer(k):
        to = (x + k) % 4
        return to, (y * 8 + z_lo * 4 + to, gy)

    def y_peer(k):
        to = (y + k) % 4
        return to, (to * 8 + z_lo * 4 + x, gy)

    def z_peer(k):
        to = (z + k) % 8
        lo, hi = to % 2, to // 2
        return lo * 4 + hi, (y * 8 + lo * 4 + x, hi * 2 + core)

    nxt = ((gx + 1, gy), (gx - 1, gy), (gx, gy + 1), (gx, gy - 1))
    has = (gx < 31, gx > 0, gy < 7, gy > 0)

    loads = [
        pltpu.make_async_copy(src, dst, in_sem.at[i])
        for i, (src, dst) in enumerate(
            (
                (nodes_h, loc),
                (edges_h, edges),
                (ew1_h, ew1),
                (ew2_h, ew2),
                (nw1_h, nw1),
                (nw2_h, nw2),
                (cotn_h, cotn),
                (cote_h, cote),
                (nodes_h, ext.at[pl.ds(0, 2)]),
            )
        )
    ]
    for load in loads:
        load.start()

    barrier = pltpu.get_barrier_semaphore()
    fixed = [other]
    fixed += [x_peer(k)[1] for k in range(1, 4)]
    fixed += [y_peer(k)[1] for k in range(1, 4)]
    fixed += [z_peer(k)[1] for k in range(1, 8)]
    for q in range(4):

        @pl.when(has[q])
        def _():
            pl.semaphore_signal(barrier, inc=1, device_id=nxt[q], device_id_type=MESH)

    for peer in fixed:
        pl.semaphore_signal(barrier, inc=1, device_id=peer, device_id_type=MESH)

    loads[0].wait()
    for q in range(4):
        for s in range(2):
            pack[q, s] = loc[list_s[0, 0, q, s]]

    peers = len(fixed)
    for flag in has:
        peers += jnp.where(flag, 1, 0)
    pl.semaphore_wait(barrier, peers)

    def remote(src, dst, send, recv, to):
        return pltpu.make_async_remote_copy(
            src_ref=src, dst_ref=dst, send_sem=send, recv_sem=recv,
            device_id=to, device_id_type=MESH,
        )

    halo = [
        remote(pack.at[q], ext.at[pl.ds(2 + 2 * q, 2)], hs_sem.at[q], hr_sem.at[q], nxt[q])
        for q in range(4)
    ]
    for q in range(4):

        @pl.when(has[q])
        def _():
            halo[q].start()

    loads[1].wait()
    loads[2].wait()
    lane = lax.broadcasted_iota(jnp.int32, (Q, Q), 0)

    def before(i, c):
        rows = pl.ds(i * H, H)
        for u in range(2):
            t = 2 * i + u
            hot = picked(lane == perm_ref[0, 0, pl.ds(t, 1), :])
            pt[t] = hot.astype(BF16)
            pm[t] = hot.T.astype(BF16)
            hr[pl.ds(t * Q, Q), :] = loc[recv_s[0, 0, t]]
        aff[rows, :] = (
            dot(edges[rows, :], ew1[pl.ds(0, D), :])
            + dot(hr[rows, :], ew1[pl.ds(D, D), :])
            + eb1[...]
        )
        return c

    for q in range(4):

        @pl.when(has[q])
        def _():
            halo[q].wait_send()

    lax.fori_loop(0, 3, before, 0)
    agg[...] = jnp.zeros_like(agg)
    for load in loads[3:]:
        load.wait()
    came = (gx > 0, gx < 31, gy > 0, gy < 7)
    for q in range(4):

        @pl.when(came[q])
        def _():
            halo[q].wait_recv()

    def forward(i, c):
        rows = pl.ds(i * H, H)
        for u in range(2):
            t = 2 * i + u
            hs[pl.ds(t * Q, Q), :] = dot(pm[t], ext[send_s[0, 0, t]]).astype(BF16)
        hidden, slope = silu_parts(aff[rows, :] + dot(hs[rows, :], ew1[pl.ds(2 * D, D), :]))
        hid[rows, :] = hidden
        aff[rows, :] = slope
        message, inv = normed_rows(dot(hidden, ew2[...]))
        msg[rows, :] = message
        einv[rows, :] = inv
        for b in range(2):
            agg[b] += message[:Q] * picked(recv_s[0, 0, 2 * i] == b) + message[Q:] * picked(
                recv_s[0, 0, 2 * i + 1] == b
            )
        return c

    lax.fori_loop(0, 3, forward, 0)

    mine_cols = pl.ds(pl.multiple_of(core * H, H), H)
    their_cols = pl.ds(pl.multiple_of((1 - core) * H, H), H)
    for b in range(2):
        nin[pl.ds(b * Q, Q), pl.ds(0, D)] = loc[b]
        nin[pl.ds(b * Q, Q), pl.ds(D, D)] = agg[b].astype(BF16)
    nhid, nslope = silu_parts(dot(nin[...], nw1[...]) + nb1[...])
    nmsg, ninv = normed_rows(dot(nhid, nw2[...]))
    nout[...] = (nin[:, :D].astype(F32) + nmsg).astype(BF16)
    out_node = pltpu.make_async_copy(nout, nout_h, out_sem.at[0])
    out_node.start()
    gnl = norm_back(nmsg, ninv, cotn[...].astype(F32)).astype(BF16)
    gel_p[pl.ds(0, H), :] = gnl
    gnl_p[:, pl.ds(0, H)] = gel_p[pl.ds(0, H), their_cols]
    gnl_p[:, pl.ds(H, H)] = gel_p[pl.ds(0, H), mine_cols]
    gna = (dot_t(gnl, nw2[...]) * nslope).astype(BF16)
    gel_p[pl.ds(0, H), :] = gna
    gna_p[:, pl.ds(0, H)] = gel_p[pl.ds(0, H), their_cols]
    gna_p[:, pl.ds(H, H)] = gel_p[pl.ds(0, H), mine_cols]
    ginput = dot_t(gna, nw1[...])
    for b in range(2):
        owned[b] = ginput[b * Q : (b + 1) * Q, :D]
        gagg[b] = ginput[b * Q : (b + 1) * Q, D:]

    cores = [
        remote(
            gsend.at[pl.ds(lo, n), :], grecv.at[pl.ds(lo, n), :],
            cs_sem.at[i], cr_sem.at[i], other,
        )
        for i, (lo, n) in enumerate(PIECES)
    ]

    def put(at, value):
        gsend[pl.ds(at, H), :] = value[:, :H].astype(BF16)
        gown[pl.ds(at, H), :] = value[:, H:]

    def outer(left, right, base, blocks):
        def one(j, c):
            j = pl.multiple_of(j * H, H)
            put(base + j, t_dot(left[:, pl.ds(j, H)], right[...]))
            return c

        lax.fori_loop(0, blocks, one, 0)

    geap[pl.ds(0, H), :] = nhid
    outer_rows = geap.at[pl.ds(0, H), :]
    outer(outer_rows, gnl_p, 6 * D, 2)
    outer(nin, gna_p, 4 * D, 4)
    cores[0].start()

    def backward(i, c):
        rows = pl.ds(i * H, H)
        up = jnp.concatenate(
            [gagg[recv_s[0, 0, 2 * i]], gagg[recv_s[0, 0, 2 * i + 1]]], axis=0
        ) + cote[rows, :].astype(F32)
        gel = norm_back(msg[rows, :], einv[rows, :], up).astype(BF16)
        gea[rows, :] = gel
        gel_p[rows, pl.ds(0, H)] = gea[rows, their_cols]
        gel_p[rows, pl.ds(H, H)] = gea[rows, mine_cols]
        gea[rows, :] = (dot_t(gel, ew2[...]) * aff[rows, :]).astype(BF16)
        geap[rows, pl.ds(0, H)] = gea[rows, their_cols]
        geap[rows, pl.ds(H, H)] = gea[rows, mine_cols]
        return c

    lax.fori_loop(0, 3, backward, 0)
    outer(hid, gel_p, 3 * D, 2)
    cores[1].start()

    def pair_sum(lo, hi):
        def one(j, c):
            rows = pl.ds(pl.multiple_of(j * BLK, 16), BLK)
            total = (gown[rows, :] + grecv[rows, :].astype(F32)).astype(BF16)
            g1a[j // 4, j % 4] = total[:, :Q]
            g1b[j // 4, j % 4] = total[:, Q:]
            return c

        lax.fori_loop(lo, hi, one, 0)

    early, late, sides = [], [], []
    for k in range(1, 4):
        to, who = x_peer(k)
        for got, lo, n, sem in ((early, EARLY, NGROUP - EARLY, 0), (late, 0, EARLY, 3)):
            got.append(
                remote(
                    g1a.at[pl.ds(lo, n), to], r1a.at[k - 1, pl.ds(lo, n)],
                    as_sem.at[sem + k - 1], ar_sem.at[sem + k - 1], who,
                )
            )
        to, who = y_peer(k)
        sides.append(
            remote(
                g1b.at[pl.ds(2 * to, 2)], r1b.at[k - 1],
                ys_sem.at[k - 1], yr_sem.at[k - 1], who,
            )
        )

    cores[0].wait_recv()
    pair_sum(4 * EARLY, 32)
    for copy in early:
        copy.start()

    outer(edges, geap, 0, 2)
    cores[2].start()
    outer(hr, geap, D, 2)
    cores[3].start()
    outer(hs, geap, 2 * D, 2)
    cores[4].start()
    for copy in cores[1:]:
        copy.wait_recv()
    pair_sum(0, 4 * EARLY)
    for copy in sides:
        copy.start()
    for copy in late:
        copy.start()

    def inputs(i, c):
        rows = pl.ds(i * H, H)
        part = gea[rows, :]
        egrad[rows, :] = (
            cote[rows, :].astype(F32) + dot_t(part, ew1[pl.ds(0, D), :])
        ).astype(BF16)
        grad_r = dot_t(part, ew1[pl.ds(D, D), :])
        for b in range(2):
            owned[b] += grad_r[:Q] * picked(recv_s[0, 0, 2 * i] == b) + grad_r[Q:] * picked(
                recv_s[0, 0, 2 * i + 1] == b
            )
        for u in range(2):
            t = 2 * i + u
            rows_t = pl.ds(t * Q, Q)
            hs[rows_t, :] = dot(pt[t], gea[rows_t, :]).astype(BF16)
        grad_s = dot_t(hs[rows, :], ew1[pl.ds(2 * D, D), :])
        for u in range(2):
            xs[2 * i + u] = grad_s[u * Q : (u + 1) * Q]
        return c

    lax.fori_loop(0, 3, inputs, 0)
    out_edge = pltpu.make_async_copy(egrad, egrad_h, out_sem.at[1])
    out_edge.start()

    def slots(b, c):
        total = xs[0] * picked(send_s[0, 0, 0] == b + 2)
        for t in range(1, 6):
            total += xs[t] * picked(send_s[0, 0, t] == b + 2)
        hret[b // 2, b % 2] = total.astype(BF16)
        return c

    lax.fori_loop(0, 8, slots, 0)
    back = (nxt[1], nxt[0], nxt[3], nxt[2])
    home = [
        remote(hret.at[q], ret.at[q], bs_sem.at[q], br_sem.at[q], back[q]) for q in range(4)
    ]
    for q in range(4):

        @pl.when(came[q])
        def _():
            home[q].start()

    for b in range(2):
        total = owned[b] + cotn[pl.ds(b * Q, Q), :].astype(F32)
        for t in range(6):
            total += xs[t] * picked(send_s[0, 0, t] == b)
        owned[b] = total

    for copy in early + late:
        copy.wait_recv()

    def sum_a(g, c):
        total = g1a[g, x].astype(F32)
        for k in range(3):
            total += r1a[k, g].astype(F32)
        g2a[g // 2, g % 2] = total.astype(BF16)
        return c

    lax.fori_loop(0, NGROUP, sum_a, 0)
    second_a, second_b = [], []
    for k in range(1, 4):
        to, who = y_peer(k)
        second_a.append(
            remote(g2a.at[to], r2a.at[k - 1], a2s_sem.at[k - 1], a2r_sem.at[k - 1], who)
        )
        to, who = x_peer(k)
        second_b.append(
            remote(g2b.at[to], r2b.at[k - 1], b2s_sem.at[k - 1], b2r_sem.at[k - 1], who)
        )
    for copy in second_a:
        copy.start()
    for copy in sides:
        copy.wait_recv()

    def sum_b(j, c):
        total = g1b[2 * y + j // 4, j % 4].astype(F32)
        for k in range(3):
            total += r1b[k, j // 4, j % 4].astype(F32)
        g2b[j % 4, j // 4] = total.astype(BF16)
        return c

    lax.fori_loop(0, NGROUP, sum_b, 0)
    for copy in second_b:
        copy.start()

    for copy in second_a + second_b:
        copy.wait_recv()
    for g in range(2):
        total = g2a[y, g].astype(F32)
        for k in range(3):
            total += r2a[k, g].astype(F32)
        g3[g, pl.ds(0, BLK), pl.ds(0, Q)] = total
        total = g2b[x, g].astype(F32)
        for k in range(3):
            total += r2b[k, g].astype(F32)
        g3[g, pl.ds(0, BLK), pl.ds(Q, Q)] = total
        g3[g, pl.ds(BLK, 16), :] = jnp.zeros((16, H), F32)
        for h in range(4):
            s3[4 * g + h] = g3[g, pl.ds(CHIP_ROWS * h, 32), :].astype(BF16)
    along = []
    for k in range(1, 8):
        to, who = z_peer(k)
        along.append(
            remote(s3.at[to], r3.at[k - 1], zs_sem.at[k - 1], zr_sem.at[k - 1], who)
        )
    for copy in along:
        copy.start()

    has_home = has
    for q in range(4):

        @pl.when(has_home[q])
        def _():
            home[q].wait_recv()

    for b in range(2):
        total = owned[b]
        for q in range(4):
            for s in range(2):
                wanted = jnp.logical_and(list_s[0, 0, q, s] == b, count_s[0, 0, q] > s)
                weight = jnp.where(wanted, 1, 0) * jnp.ones((Q, D), jnp.int32)
                total += jnp.where(weight > 0, ret[q, s].astype(F32), 0.0)
        ngrad[pl.ds(b * Q, Q), :] = total.astype(BF16)
    out_grad = pltpu.make_async_copy(ngrad, ngrad_h, out_sem.at[2])
    out_grad.start()

    for copy in along:
        copy.wait_recv()
    total = s3[z_lo * 4 + z_hi].astype(F32)
    for k in range(7):
        total += r3[k].astype(F32)
    fin[...] = total

    first = fin[pl.ds(0, 16), :]
    second = fin[pl.ds(14, 16), :]
    swap_s[...] = jnp.where(core == 0, second, first)
    swap = remote(swap_s, swap_r, ws_sem, wr_sem, other)
    swap.start()

    local = lax.broadcasted_iota(jnp.int32, (32, H), 0)
    row = local + CHIP_ROWS * (gx * 4 + z_hi)
    square = jnp.where(local < CHIP_ROWS, total * total, 0.0)
    square = square[:, :Q] + square[:, Q:]
    row = row[:, :Q]
    cuts = (0,) + BOUNDS + (ROWS,)
    pieces = [
        jnp.sum(
            jnp.where(jnp.logical_and(row >= cuts[m], row < cuts[m + 1]), square, 0.0),
            axis=0, keepdims=True,
        )
        for m in range(4)
    ]
    stat = jnp.concatenate(pieces + [jnp.zeros((4, Q), F32)], axis=0)
    rounds = (
        [other],
        [z_peer(k)[1] for k in range(1, 8)],
        [x_peer(k)[1] for k in range(1, 4)],
        [y_peer(k)[1] for k in range(1, 4)],
    )
    at = 0
    stat_copies = []
    for r, peers in enumerate(rounds):
        stat_s[r] = stat
        now = [
            remote(stat_s.at[r], stat_r.at[at + i], ts_sem.at[at + i], tr_sem.at[at + i], who)
            for i, who in enumerate(peers)
        ]
        for copy in now:
            copy.start()
        for copy in now:
            copy.wait_recv()
        for i in range(len(peers)):
            stat = stat + stat_r[at + i]
        at += len(peers)
        stat_copies += now

    swap.wait_recv()
    keep = jnp.where(core == 0, first, second)
    scales = [
        lax.rsqrt(jnp.sum(stat[m : m + 1], axis=-1, keepdims=True) * (1.0 / SIZES[m]) + 1e-06)
        for m in range(4)
    ]
    row = lax.broadcasted_iota(jnp.int32, (16, H), 0) + 14 * (gx * 8 + gy)
    scale = jnp.where(
        row < BOUNDS[0],
        scales[0],
        jnp.where(row < BOUNDS[1], scales[1], jnp.where(row < BOUNDS[2], scales[2], scales[3])),
    )
    theirs = swap_r[...]
    left = jnp.where(core == 0, keep, theirs) * scale
    right = jnp.where(core == 0, theirs, keep) * scale
    for g in range(2):
        flat[pl.ds(g, 16, stride=4), :] = left[:, g * Q : (g + 1) * Q]
        flat[pl.ds(2 + g, 16, stride=4), :] = right[:, g * Q : (g + 1) * Q]
    wdir[...] = flat[pl.ds(0, 56), :].astype(BF16)

    for q in range(4):

        @pl.when(came[q])
        def _():
            home[q].wait_send()

    for copy in cores + early + late + sides + second_a + second_b + along + stat_copies:
        copy.wait_send()
    swap.wait_send()
    out_node.wait()
    out_edge.wait()
    out_grad.wait()


def on_device(
    node_latents, edge_latents, edge_w1, edge_b1, edge_w2, node_w1, node_b1, node_w2,
    node_cot, edge_cot, send_count, send_list, tile_recv, tile_send, tile_perm,
):
    hbm = pl.BlockSpec(memory_space=pl.ANY)
    vmem = pl.BlockSpec(memory_space=pltpu.VMEM)
    smem = pl.BlockSpec(memory_space=pltpu.SMEM)
    b = functools.partial(pltpu.VMEM, dtype=BF16)
    f = functools.partial(pltpu.VMEM, dtype=F32)
    sem = lambda n: pltpu.SemaphoreType.DMA((n,))
    one = pltpu.SemaphoreType.DMA
    scratch = [
        b((2, Q, D)), b((10, Q, D)), b((768, D)), b((3 * D, D)), b((D, D)), b((2 * D, D)), b((D, D)),
        b((H, D)), b((768, D)), b((4, 2, Q, D)), b((6, Q, Q)), b((6, Q, Q)),
        b((768, D)), b((768, D)), f((768, D)), b((768, D)), f((768, D)), f((768, 1)),
        f((2, Q, D)), f((2, Q, D)), f((2, Q, D)), b((768, D)), b((768, D)), b((768, D)),
        b((H, 2 * D)), b((H, D)), b((H, D)), f((6, Q, D)), b((4, 2, Q, D)), b((4, 2, Q, D)),
        b((H, D)), b((H, D)), b((768, D)),
        b((ROWS, H)), f((ROWS, H)), b((ROWS, H)),
        b((8, 4, BLK, Q)), b((8, 4, BLK, Q)), b((3, 8, BLK, Q)), b((3, 2, 4, BLK, Q)),
        b((4, 2, BLK, Q)), b((4, 2, BLK, Q)), b((3, 2, BLK, Q)), b((3, 2, BLK, Q)),
        f((2, Q, H)), b((8, 32, H)), b((7, 32, H)), f((32, H)), f((16, H)), f((16, H)),
        f((4, 8, Q)), f((14, 8, Q)), f((64, Q)),
        sem(9), sem(3), sem(4), sem(4), sem(4), sem(4), sem(5), sem(5),
        sem(6), sem(6), sem(3), sem(3), sem(3), sem(3), sem(3), sem(3),
        sem(7), sem(7), one, one, sem(14), sem(14),
    ]
    nout, ngrad, egrad, wdir = pl.pallas_call(
        kernel,
        out_shape=(
            jax.ShapeDtypeStruct((H, D), BF16),
            jax.ShapeDtypeStruct((H, D), BF16),
            jax.ShapeDtypeStruct((768, D), BF16),
            jax.ShapeDtypeStruct((56, Q), BF16),
        ),
        in_specs=[smem] * 4 + [vmem] * 3 + [hbm] * 8,
        out_specs=(hbm, hbm, hbm, vmem),
        scratch_shapes=scratch,
        compiler_params=pltpu.CompilerParams(
            collective_id=0, has_side_effects=True, vmem_limit_bytes=56 * 1024 * 1024
        ),
        name="layer",
    )(
        send_count, send_list, tile_recv, tile_send, tile_perm,
        edge_b1.reshape(1, D), node_b1.reshape(1, D),
        node_latents.reshape(2, Q, D), edge_latents.reshape(768, D),
        edge_w1, edge_w2, node_w1, node_w2,
        node_cot.reshape(H, D), edge_cot.reshape(768, D),
    )
    return (
        nout.reshape(1, 1, H, D),
        ngrad.reshape(1, 1, H, D),
        egrad.reshape(1, 1, 768, D),
        wdir.reshape(7168),
    )


def solution(mesh):
    cells = P("gx", "gy", None, None)
    flat = P("gx", "gy", None)
    return jax.shard_map(
        on_device,
        mesh=mesh,
        in_specs=(
            cells, cells, P(), P(), P(), P(), P(), P(), cells, cells,
            flat, cells, flat, flat, cells,
        ),
        out_specs=(cells, cells, cells, P(("gx", "gy"))),
        check_vma=False,
    )
```

```python
import functools

import jax
import jax.numpy as jnp
from jax import lax
from jax.experimental import pallas as pl
from jax.experimental.pallas import tpu as pltpu
from jax.sharding import PartitionSpec as P

MESH = pl.DeviceIdType.MESH
F32 = jnp.float32
BF16 = jnp.bfloat16
D = 512
H = 256
Q = 128
ROWS = 7 * D
CHIP_ROWS = 28
BLK = 112
NGROUP = 8
EARLY = 5
BOUNDS = (3 * D, 4 * D, 6 * D)
SIZES = (3 * D * D, D * D, 2 * D * D, D * D)
PIECES = ((4 * D, 3 * D), (3 * D, D), (0, D), (D, D), (2 * D, D))


def dot(a, b):
    return jnp.dot(a, b, preferred_element_type=F32)


def dot_t(a, b):
    return lax.dot_general(a, b, (((1,), (1,)), ((), ())), preferred_element_type=F32)


def t_dot(a, b):
    return lax.dot_general(a, b, (((0,), (0,)), ((), ())), preferred_element_type=F32)


def normed_rows(values):
    center = values - jnp.mean(values, axis=-1, keepdims=True)
    inv = lax.rsqrt(jnp.mean(center * center, axis=-1, keepdims=True) + 1e-05)
    return center * inv, inv


def norm_back(normed, inv, up):
    return inv * (
        up
        - jnp.mean(up, axis=-1, keepdims=True)
        - normed * jnp.mean(up * normed, axis=-1, keepdims=True)
    )


def silu_parts(v):
    s = jax.nn.sigmoid(v)
    return (v * s).astype(BF16), s * (1.0 + v * (1.0 - s))


def picked(flag):
    return jnp.where(flag, 1.0, 0.0).astype(F32)


def kernel(
    count_s, list_s, recv_s, send_s, perm_ref, eb1, nb1,
    nodes_h, edges_h, ew1_h, ew2_h, nw1_h, nw2_h, cotn_h, cote_h,
    nout_h, ngrad_h, egrad_h, wdir,
    loc, ext, edges, ew1, ew2, nw1, nw2, cotn, cote, pack, pt, pm,
    hr, hs, aff, hid, msg, einv, agg, gagg, owned, gea, geap, gel_p,
    nin, gna_p, gnl_p, xs, hret, ret, nout, ngrad, egrad,
    gsend, gown, grecv, g1a, g1b, r1a, r1b, g2a, g2b, r2a, r2b,
    g3, s3, r3, fin, swap_s, swap_r, stat_s, stat_r, flat,
    in_sem, out_sem, hs_sem, hr_sem, bs_sem, br_sem, cs_sem, cr_sem,
    as_sem, ar_sem, ys_sem, yr_sem, a2s_sem, a2r_sem, b2s_sem, b2r_sem,
    zs_sem, zr_sem, ws_sem, wr_sem, ts_sem, tr_sem,
):
    gx = lax.axis_index("gx")
    gy = lax.axis_index("gy")
    y = gx // 8
    z_lo = (gx // 4) % 2
    x = gx % 4
    z_hi = gy // 2
    core = gy % 2
    z = z_hi * 2 + z_lo
    other = (gx, z_hi * 2 + (1 - core))

    def x_peer(k):
        to = (x + k) % 4
        return to, (y * 8 + z_lo * 4 + to, gy)

    def y_peer(k):
        to = (y + k) % 4
        return to, (to * 8 + z_lo * 4 + x, gy)

    def z_peer(k):
        to = (z + k) % 8
        lo, hi = to % 2, to // 2
        return lo * 4 + hi, (y * 8 + lo * 4 + x, hi * 2 + core)

    own_blk = z_lo * 16 + ((y + 4 - x) % 4) * 4 + x
    from_gx = ((gx // 4 + x) % 4) * 8 + (gx // 16) * 4 + x

    nxt = ((gx + 1, gy), (gx - 1, gy), (gx, gy + 1), (gx, gy - 1))
    has = (gx < 31, gx > 0, gy < 7, gy > 0)

    loads = [
        pltpu.make_async_copy(src, dst, in_sem.at[i])
        for i, (src, dst) in enumerate(
            (
                (nodes_h, loc),
                (edges_h, edges),
                (ew1_h, ew1),
                (ew2_h, ew2),
                (nw1_h, nw1),
                (nw2_h, nw2),
                (cotn_h, cotn),
                (cote_h, cote),
                (nodes_h, ext.at[pl.ds(0, 2)]),
            )
        )
    ]
    for load in loads:
        load.start()

    barrier = pltpu.get_barrier_semaphore()
    fixed = [other]
    fixed += [x_peer(k)[1] for k in range(1, 4)]
    fixed += [y_peer(k)[1] for k in range(1, 4)]
    fixed += [z_peer(k)[1] for k in range(1, 8)]
    for q in range(4):

        @pl.when(has[q])
        def _():
            pl.semaphore_signal(barrier, inc=1, device_id=nxt[q], device_id_type=MESH)

    for peer in fixed:
        pl.semaphore_signal(barrier, inc=1, device_id=peer, device_id_type=MESH)

    loads[0].wait()
    for q in range(4):
        for s in range(2):
            pack[q, s] = loc[list_s[0, 0, s, q]]

    peers = len(fixed)
    for flag in has:
        peers += jnp.where(flag, 1, 0)
    pl.semaphore_wait(barrier, peers)

    def remote(src, dst, send, recv, to):
        return pltpu.make_async_remote_copy(
            src_ref=src, dst_ref=dst, send_sem=send, recv_sem=recv,
            device_id=to, device_id_type=MESH,
        )

    halo = [
        remote(pack.at[q], ext.at[pl.ds(2 + 2 * q, 2)], hs_sem.at[q], hr_sem.at[q], nxt[q])
        for q in range(4)
    ]
    for q in range(4):

        @pl.when(has[q])
        def _():
            halo[q].start()

    loads[1].wait()
    loads[2].wait()
    lane = lax.broadcasted_iota(jnp.int32, (Q, Q), 0)

    def before(i, c):
        rows = pl.ds(i * H, H)
        for u in range(2):
            t = 2 * i + u
            hot = picked(lane == perm_ref[0, t])
            pt[t] = hot.astype(BF16)
            pm[t] = hot.T.astype(BF16)
            hr[pl.ds(t * Q, Q), :] = loc[recv_s[0, 0, t]]
        aff[rows, :] = (
            dot(edges[rows, :], ew1[pl.ds(0, D), :])
            + dot(hr[rows, :], ew1[pl.ds(D, D), :])
            + eb1[...]
        )
        return c

    for q in range(4):

        @pl.when(has[q])
        def _():
            halo[q].wait_send()

    lax.fori_loop(0, 3, before, 0)
    agg[...] = jnp.zeros_like(agg)
    for load in loads[3:]:
        load.wait()
    came = (gx > 0, gx < 31, gy > 0, gy < 7)
    for q in range(4):

        @pl.when(came[q])
        def _():
            halo[q].wait_recv()

    def forward(i, c):
        rows = pl.ds(i * H, H)
        for u in range(2):
            t = 2 * i + u
            hs[pl.ds(t * Q, Q), :] = dot(pm[t], ext[send_s[0, 0, t]]).astype(BF16)
        hidden, slope = silu_parts(aff[rows, :] + dot(hs[rows, :], ew1[pl.ds(2 * D, D), :]))
        hid[rows, :] = hidden
        aff[rows, :] = slope
        message, inv = normed_rows(dot(hidden, ew2[...]))
        msg[rows, :] = message
        einv[rows, :] = inv
        for b in range(2):
            agg[b] += message[:Q] * picked(recv_s[0, 0, 2 * i] == b) + message[Q:] * picked(
                recv_s[0, 0, 2 * i + 1] == b
            )
        return c

    lax.fori_loop(0, 3, forward, 0)

    mine_cols = pl.ds(pl.multiple_of(core * H, H), H)
    their_cols = pl.ds(pl.multiple_of((1 - core) * H, H), H)
    for b in range(2):
        nin[pl.ds(b * Q, Q), pl.ds(0, D)] = loc[b]
        nin[pl.ds(b * Q, Q), pl.ds(D, D)] = agg[b].astype(BF16)
    nhid, nslope = silu_parts(dot(nin[...], nw1[...]) + nb1[...])
    nmsg, ninv = normed_rows(dot(nhid, nw2[...]))
    nout[...] = (nin[:, :D].astype(F32) + nmsg).astype(BF16)
    out_node = pltpu.make_async_copy(nout, nout_h, out_sem.at[0])
    out_node.start()
    gnl = norm_back(nmsg, ninv, cotn[...].astype(F32)).astype(BF16)
    gel_p[pl.ds(0, H), :] = gnl
    gnl_p[:, pl.ds(0, H)] = gel_p[pl.ds(0, H), their_cols]
    gnl_p[:, pl.ds(H, H)] = gel_p[pl.ds(0, H), mine_cols]
    gna = (dot_t(gnl, nw2[...]) * nslope).astype(BF16)
    gel_p[pl.ds(0, H), :] = gna
    gna_p[:, pl.ds(0, H)] = gel_p[pl.ds(0, H), their_cols]
    gna_p[:, pl.ds(H, H)] = gel_p[pl.ds(0, H), mine_cols]
    ginput = dot_t(gna, nw1[...])
    for b in range(2):
        owned[b] = ginput[b * Q : (b + 1) * Q, :D]
        gagg[b] = ginput[b * Q : (b + 1) * Q, D:]

    cores = [
        remote(
            gsend.at[pl.ds(lo, n), :], grecv.at[pl.ds(lo, n), :],
            cs_sem.at[i], cr_sem.at[i], other,
        )
        for i, (lo, n) in enumerate(PIECES)
    ]

    def put(at, value):
        gsend[pl.ds(at, H), :] = value[:, :H].astype(BF16)
        gown[pl.ds(at, H), :] = value[:, H:]

    def outer(left, right, base, blocks):
        def one(j, c):
            j = pl.multiple_of(j * H, H)
            put(base + j, t_dot(left[:, pl.ds(j, H)], right[...]))
            return c

        lax.fori_loop(0, blocks, one, 0)

    geap[pl.ds(0, H), :] = nhid
    outer_rows = geap.at[pl.ds(0, H), :]
    outer(outer_rows, gnl_p, 6 * D, 2)
    outer(nin, gna_p, 4 * D, 4)
    cores[0].start()

    def backward(i, c):
        rows = pl.ds(i * H, H)
        up = jnp.concatenate(
            [gagg[recv_s[0, 0, 2 * i]], gagg[recv_s[0, 0, 2 * i + 1]]], axis=0
        ) + cote[rows, :].astype(F32)
        gel = norm_back(msg[rows, :], einv[rows, :], up).astype(BF16)
        gea[rows, :] = gel
        gel_p[rows, pl.ds(0, H)] = gea[rows, their_cols]
        gel_p[rows, pl.ds(H, H)] = gea[rows, mine_cols]
        gea[rows, :] = (dot_t(gel, ew2[...]) * aff[rows, :]).astype(BF16)
        geap[rows, pl.ds(0, H)] = gea[rows, their_cols]
        geap[rows, pl.ds(H, H)] = gea[rows, mine_cols]
        return c

    lax.fori_loop(0, 3, backward, 0)
    outer(hid, gel_p, 3 * D, 2)
    cores[1].start()

    def pair_sum(lo, hi):
        def one(j, c):
            rows = pl.ds(pl.multiple_of(j * BLK, 16), BLK)
            total = (gown[rows, :] + grecv[rows, :].astype(F32)).astype(BF16)
            g1a[j // 4, j % 4] = total[:, :Q]
            g1b[j // 4, (j // 4 + j) % 4] = total[:, Q:]
            return c

        lax.fori_loop(lo, hi, one, 0)

    early, late = [], []
    for got, lo, n, sem in ((early, EARLY, NGROUP - EARLY, 0), (late, 0, EARLY, 3)):
        for k in range(1, 4):
            to, who = x_peer(k)
            got.append(
                remote(
                    g1a.at[pl.ds(lo, n), to], r1a.at[k - 1, pl.ds(lo, n)],
                    as_sem.at[sem + k - 1], ar_sem.at[sem + k - 1], who,
                )
            )
            to, who = y_peer(k)
            got.append(
                remote(
                    g1b.at[pl.ds(lo, n), to], r1b.at[k - 1, pl.ds(lo, n)],
                    ys_sem.at[sem + k - 1], yr_sem.at[sem + k - 1], who,
                )
            )

    cores[0].wait_recv()
    pair_sum(4 * EARLY, 32)
    for copy in early:
        copy.start()

    outer(edges, geap, 0, 2)
    cores[2].start()
    outer(hr, geap, D, 2)
    cores[3].start()
    outer(hs, geap, 2 * D, 2)
    cores[4].start()
    for copy in cores[1:]:
        copy.wait_recv()
    pair_sum(0, 4 * EARLY)
    for copy in late:
        copy.start()

    def inputs(i, c):
        rows = pl.ds(i * H, H)
        part = gea[rows, :]
        egrad[rows, :] = (
            cote[rows, :].astype(F32) + dot_t(part, ew1[pl.ds(0, D), :])
        ).astype(BF16)
        grad_r = dot_t(part, ew1[pl.ds(D, D), :])
        for b in range(2):
            owned[b] += grad_r[:Q] * picked(recv_s[0, 0, 2 * i] == b) + grad_r[Q:] * picked(
                recv_s[0, 0, 2 * i + 1] == b
            )
        for u in range(2):
            t = 2 * i + u
            rows_t = pl.ds(t * Q, Q)
            hs[rows_t, :] = dot(pt[t], gea[rows_t, :]).astype(BF16)
        grad_s = dot_t(hs[rows, :], ew1[pl.ds(2 * D, D), :])
        for u in range(2):
            xs[2 * i + u] = grad_s[u * Q : (u + 1) * Q]
        return c

    lax.fori_loop(0, 3, inputs, 0)
    out_edge = pltpu.make_async_copy(egrad, egrad_h, out_sem.at[1])
    out_edge.start()

    def slots(b, c):
        total = xs[0] * picked(send_s[0, 0, 0] == b + 2)
        for t in range(1, 6):
            total += xs[t] * picked(send_s[0, 0, t] == b + 2)
        hret[b // 2, b % 2] = total.astype(BF16)
        return c

    lax.fori_loop(0, 8, slots, 0)
    back = (nxt[1], nxt[0], nxt[3], nxt[2])
    home = [
        remote(hret.at[q], ret.at[q], bs_sem.at[q], br_sem.at[q], back[q]) for q in range(4)
    ]
    for q in range(4):

        @pl.when(came[q])
        def _():
            home[q].start()

    for b in range(2):
        total = owned[b] + cotn[pl.ds(b * Q, Q), :].astype(F32)
        for t in range(6):
            total += xs[t] * picked(send_s[0, 0, t] == b)
        owned[b] = total

    def sum_first(g, c):
        total = g1a[g, x].astype(F32)
        for k in range(3):
            total += r1a[k, g].astype(F32)
        g2a[(g + x) % 4, g // 4] = total.astype(BF16)
        total = g1b[g, y].astype(F32)
        for k in range(3):
            total += r1b[k, g].astype(F32)
        g2b[(y + 8 - g) % 4, g // 4] = total.astype(BF16)
        return c

    for copy in early:
        copy.wait_recv()
    lax.fori_loop(EARLY, NGROUP, sum_first, 0)
    for copy in late:
        copy.wait_recv()
    lax.fori_loop(0, EARLY, sum_first, 0)
    second = []
    for k in range(1, 4):
        to, who = y_peer(k)
        second.append(
            remote(g2a.at[to], r2a.at[k - 1], a2s_sem.at[k - 1], a2r_sem.at[k - 1], who)
        )
        to, who = x_peer(k)
        second.append(
            remote(g2b.at[to], r2b.at[k - 1], b2s_sem.at[k - 1], b2r_sem.at[k - 1], who)
        )
    for copy in second:
        copy.start()

    for copy in second:
        copy.wait_recv()
    for g in range(2):
        total = g2a[y, g].astype(F32)
        for k in range(3):
            total += r2a[k, g].astype(F32)
        g3[g, pl.ds(0, BLK), pl.ds(0, Q)] = total
        total = g2b[x, g].astype(F32)
        for k in range(3):
            total += r2b[k, g].astype(F32)
        g3[g, pl.ds(0, BLK), pl.ds(Q, Q)] = total
        g3[g, pl.ds(BLK, 16), :] = jnp.zeros((16, H), F32)
        for h in range(4):
            s3[4 * g + h] = g3[g, pl.ds(CHIP_ROWS * h, 32), :].astype(BF16)
    along = []
    for k in range(1, 8):
        to, who = z_peer(k)
        along.append(
            remote(s3.at[to], r3.at[k - 1], zs_sem.at[k - 1], zr_sem.at[k - 1], who)
        )
    for copy in along:
        copy.start()

    for copy in along:
        copy.wait_recv()
    total = s3[z_lo * 4 + z_hi].astype(F32)
    for k in range(7):
        total += r3[k].astype(F32)
    fin[...] = total

    def node_gradient():
        for q in range(4):

            @pl.when(has[q])
            def _():
                home[q].wait_recv()

        for b in range(2):
            total = owned[b]
            for q in range(4):
                for s in range(2):
                    wanted = jnp.logical_and(list_s[0, 0, s, q] == b, count_s[0, 0, q] > s)
                    weight = jnp.where(wanted, 1, 0) * jnp.ones((Q, D), jnp.int32)
                    total += jnp.where(weight > 0, ret[q, s].astype(F32), 0.0)
            ngrad[pl.ds(b * Q, Q), :] = total.astype(BF16)
        out_grad = pltpu.make_async_copy(ngrad, ngrad_h, out_sem.at[2])
        out_grad.start()
        return out_grad

    swap_s[0] = fin[pl.ds(0, 16), :]
    swap_s[1] = fin[pl.ds(14, 16), :]
    swap = [
        remote(swap_s.at[c], swap_r.at[core], ws_sem.at[c], wr_sem.at[core], (own_blk, z_hi * 2 + c))
        for c in range(2)
    ]
    stay = pltpu.make_async_copy(swap_s.at[core], swap_r.at[core], in_sem.at[0])
    for c in range(2):

        @pl.when(jnp.logical_or(own_blk != gx, core != c))
        def _():
            swap[c].start()

    @pl.when(own_blk == gx)
    def _():
        stay.start()

    local = lax.broadcasted_iota(jnp.int32, (32, H), 0)
    row = local + CHIP_ROWS * (own_blk * 4 + z_hi)
    square = jnp.where(local < CHIP_ROWS, total * total, 0.0)
    square = square[:, :Q] + square[:, Q:]
    row = row[:, :Q]
    cuts = (0,) + BOUNDS + (ROWS,)
    pieces = [
        jnp.sum(
            jnp.where(jnp.logical_and(row >= cuts[m], row < cuts[m + 1]), square, 0.0),
            axis=0, keepdims=True,
        )
        for m in range(4)
    ]
    stat = jnp.concatenate(pieces + [jnp.zeros((4, Q), F32)], axis=0)
    rounds = ([], [])
    for k in range(1, 16):
        to = (z + k % 8) % 8
        rounds[0].append((y * 8 + (to % 2) * 4 + x, (to // 2) * 2 + (core + k // 8) % 2))
        rounds[1].append((((y + k // 4) % 4) * 8 + z_lo * 4 + (x + k % 4) % 4, gy))
    stat_copies = []
    for r, peers in enumerate(rounds):
        stat_s[r] = stat
        now = [
            remote(stat_s.at[r], stat_r.at[15 * r + i], ts_sem.at[15 * r + i], tr_sem.at[15 * r + i], who)
            for i, who in enumerate(peers)
        ]
        for copy in now:
            copy.start()
        if r == 1:
            out_grad = node_gradient()
        for copy in now:
            copy.wait_recv()
        for i in range(15):
            stat = stat + stat_r[15 * r + i]
        stat_copies += now

    taken = [
        remote(swap_s.at[c], swap_r.at[c], ws_sem.at[c], wr_sem.at[c], (from_gx, z_hi * 2 + c))
        for c in range(2)
    ]
    for c in range(2):

        @pl.when(jnp.logical_or(from_gx != gx, core != c))
        def _():
            taken[c].wait_recv()

    @pl.when(own_blk == gx)
    def _():
        stay.wait()

    scales = [
        lax.rsqrt(jnp.sum(stat[m : m + 1], axis=-1, keepdims=True) * (1.0 / SIZES[m]) + 1e-06)
        for m in range(4)
    ]
    row = lax.broadcasted_iota(jnp.int32, (16, H), 0) + 14 * (gx * 8 + gy)
    scale = jnp.where(
        row < BOUNDS[0],
        scales[0],
        jnp.where(row < BOUNDS[1], scales[1], jnp.where(row < BOUNDS[2], scales[2], scales[3])),
    )
    left = swap_r[0] * scale
    right = swap_r[1] * scale
    for g in range(2):
        flat[pl.ds(g, 16, stride=4), :] = left[:, g * Q : (g + 1) * Q]
        flat[pl.ds(2 + g, 16, stride=4), :] = right[:, g * Q : (g + 1) * Q]
    wdir[...] = flat[pl.ds(0, 56), :].astype(BF16)

    for q in range(4):

        @pl.when(came[q])
        def _():
            home[q].wait_send()

    for copy in cores + early + late + second + along + stat_copies:
        copy.wait_send()
    for c in range(2):

        @pl.when(jnp.logical_or(own_blk != gx, core != c))
        def _():
            swap[c].wait_send()

    out_node.wait()
    out_edge.wait()
    out_grad.wait()


def hand_over(*refs):
    sem = refs[-1]
    copies = [pltpu.make_async_copy(refs[i], refs[4 + i], sem.at[i]) for i in range(4)]
    for copy in copies:
        copy.start()
    for copy in copies:
        copy.wait()


def on_device(
    node_latents, edge_latents, edge_w1, edge_b1, edge_w2, node_w1, node_b1, node_w2,
    node_cot, edge_cot, send_count, send_list, tile_recv, tile_send, tile_perm,
):
    hbm = pl.BlockSpec(memory_space=pl.ANY)
    vmem = pl.BlockSpec(memory_space=pltpu.VMEM)
    smem = pl.BlockSpec(memory_space=pltpu.SMEM)
    b = functools.partial(pltpu.VMEM, dtype=BF16)
    f = functools.partial(pltpu.VMEM, dtype=F32)
    sem = lambda n: pltpu.SemaphoreType.DMA((n,))
    scratch = [
        b((2, Q, D)), b((10, Q, D)), b((768, D)), b((3 * D, D)), b((D, D)), b((2 * D, D)), b((D, D)),
        b((H, D)), b((768, D)), b((4, 2, Q, D)), b((6, Q, Q)), b((6, Q, Q)),
        b((768, D)), b((768, D)), f((768, D)), b((768, D)), f((768, D)), f((768, 1)),
        f((2, Q, D)), f((2, Q, D)), f((2, Q, D)), b((768, D)), b((768, D)), b((768, D)),
        b((H, 2 * D)), b((H, D)), b((H, D)), f((6, Q, D)), b((4, 2, Q, D)), b((4, 2, Q, D)),
        b((H, D)), b((H, D)), b((768, D)),
        b((ROWS, H)), f((ROWS, H)), b((ROWS, H)),
        b((8, 4, BLK, Q)), b((8, 4, BLK, Q)), b((3, 8, BLK, Q)), b((3, 8, BLK, Q)),
        b((4, 2, BLK, Q)), b((4, 2, BLK, Q)), b((3, 2, BLK, Q)), b((3, 2, BLK, Q)),
        f((2, Q, H)), b((8, 32, H)), b((7, 32, H)), f((32, H)), f((2, 16, H)), f((2, 16, H)),
        f((2, 8, Q)), f((30, 8, Q)), f((64, Q)),
        sem(9), sem(3), sem(4), sem(4), sem(4), sem(4), sem(5), sem(5),
        sem(6), sem(6), sem(6), sem(6), sem(3), sem(3), sem(3), sem(3),
        sem(7), sem(7), sem(2), sem(2), sem(30), sem(30),
    ]
    shapes = (
        jax.ShapeDtypeStruct((H, D), BF16),
        jax.ShapeDtypeStruct((H, D), BF16),
        jax.ShapeDtypeStruct((768, D), BF16),
        jax.ShapeDtypeStruct((56, Q), BF16),
    )
    results = pl.pallas_call(
        kernel,
        out_shape=shapes,
        in_specs=[smem] * 4 + [vmem] * 3 + [hbm] * 8,
        out_specs=(hbm, hbm, hbm, vmem),
        scratch_shapes=scratch,
        compiler_params=pltpu.CompilerParams(
            collective_id=0, has_side_effects=True, vmem_limit_bytes=56 * 1024 * 1024
        ),
        name="layer",
    )(
        send_count, jnp.transpose(send_list, (0, 1, 3, 2)), tile_recv, tile_send,
        jnp.transpose(tile_perm, (0, 2, 1, 3)),
        edge_b1.reshape(1, D), node_b1.reshape(1, D),
        node_latents.reshape(2, Q, D), edge_latents.reshape(768, D),
        edge_w1, edge_w2, node_w1, node_w2,
        node_cot.reshape(H, D), edge_cot.reshape(768, D),
    )
    nout, ngrad, egrad, wdir = pl.pallas_call(
        hand_over,
        out_shape=shapes,
        in_specs=[hbm] * 4,
        out_specs=(hbm,) * 4,
        scratch_shapes=[sem(4)],
        name="hand_over",
    )(*results)
    return (
        nout.reshape(1, 1, H, D),
        ngrad.reshape(1, 1, H, D),
        egrad.reshape(1, 1, 768, D),
        wdir.reshape(7168),
    )


def solution(mesh):
    cells = P("gx", "gy", None, None)
    flat = P("gx", "gy", None)
    return jax.shard_map(
        on_device,
        mesh=mesh,
        in_specs=(
            cells, cells, P(), P(), P(), P(), P(), P(), cells, cells,
            flat, cells, flat, flat, cells,
        ),
        out_specs=(cells, cells, cells, P(("gx", "gy"))),
        check_vma=False,
    )
```

```python
import functools

import jax
import jax.numpy as jnp
from jax import lax
from jax.experimental import pallas as pl
from jax.experimental.pallas import tpu as pltpu
from jax.sharding import PartitionSpec as P

MESH = pl.DeviceIdType.MESH
F32 = jnp.float32
BF16 = jnp.bfloat16
D = 512
H = 256
Q = 128
ROWS = 7 * D
CHIP_ROWS = 28
BLK = 112
NGROUP = 8
EARLY = 5
BOUNDS = (3 * D, 4 * D, 6 * D)
SIZES = (3 * D * D, D * D, 2 * D * D, D * D)
PIECES = ((4 * D, 3 * D), (3 * D, D), (0, D), (D, D), (2 * D, D))


def dot(a, b):
    return jnp.dot(a, b, preferred_element_type=F32)


def dot_t(a, b):
    return lax.dot_general(a, b, (((1,), (1,)), ((), ())), preferred_element_type=F32)


def t_dot(a, b):
    return lax.dot_general(a, b, (((0,), (0,)), ((), ())), preferred_element_type=F32)


def normed_rows(values):
    center = values - jnp.mean(values, axis=-1, keepdims=True)
    inv = lax.rsqrt(jnp.mean(center * center, axis=-1, keepdims=True) + 1e-05)
    return center * inv, inv


def norm_back(normed, inv, up):
    return inv * (
        up
        - jnp.mean(up, axis=-1, keepdims=True)
        - normed * jnp.mean(up * normed, axis=-1, keepdims=True)
    )


def silu_parts(v):
    s = jax.nn.sigmoid(v)
    return (v * s).astype(BF16), s * (1.0 + v * (1.0 - s))


def picked(flag):
    return jnp.where(flag, 1.0, 0.0).astype(F32)


def kernel(
    count_s, list_s, recv_s, send_s, perm_ref, eb1, nb1,
    nodes_h, edges_h, ew1_h, ew2_h, nw1_h, nw2_h, cotn_h, cote_h,
    nout_h, ngrad_h, egrad_h, wdir,
    loc, ext, edges, ew1, ew2, nw1, nw2, cotn, cote, pack, pt, pm,
    hr, hs, aff, hid, msg, einv, agg, gagg, owned, gea, geap, gel_p,
    nin, gna_p, gnl_p, xs, hret, ret, nout, ngrad, egrad,
    gsend, gown, grecv, g1a, g1b, r1a, r1b, g2a, g2b, r2a, r2b,
    g3, s3, r3, fin, swap_s, swap_r, stat_s, stat_r, flat,
    in_sem, out_sem, hs_sem, hr_sem, bs_sem, br_sem, cs_sem, cr_sem,
    as_sem, ar_sem, ys_sem, yr_sem, a2s_sem, a2r_sem, b2s_sem, b2r_sem,
    zs_sem, zr_sem, ws_sem, wr_sem, ts_sem, tr_sem,
):
    gx = lax.axis_index("gx")
    gy = lax.axis_index("gy")
    y = gx // 8
    z_lo = (gx // 4) % 2
    x = gx % 4
    z_hi = gy // 2
    core = gy % 2
    z = z_hi * 2 + z_lo
    other = (gx, z_hi * 2 + (1 - core))

    def x_peer(k):
        to = (x + k) % 4
        return to, (y * 8 + z_lo * 4 + to, gy)

    def y_peer(k):
        to = (y + k) % 4
        return to, (to * 8 + z_lo * 4 + x, gy)

    def z_peer(k):
        to = (z + k) % 8
        lo, hi = to % 2, to // 2
        return lo * 4 + hi, (y * 8 + lo * 4 + x, hi * 2 + core)

    own_blk = z_lo * 16 + ((y + 4 - x) % 4) * 4 + x
    from_gx = ((gx // 4 + x) % 4) * 8 + (gx // 16) * 4 + x

    nxt = ((gx + 1, gy), (gx - 1, gy), (gx, gy + 1), (gx, gy - 1))
    has = (gx < 31, gx > 0, gy < 7, gy > 0)

    loads = [
        pltpu.make_async_copy(src, dst, in_sem.at[i])
        for i, (src, dst) in enumerate(
            (
                (nodes_h, loc),
                (edges_h, edges),
                (ew1_h, ew1),
                (ew2_h, ew2),
                (nw1_h, nw1),
                (nw2_h, nw2),
                (cotn_h, cotn),
                (cote_h, cote),
                (nodes_h, ext.at[pl.ds(0, 2)]),
            )
        )
    ]
    for load in loads:
        load.start()

    barrier = pltpu.get_barrier_semaphore()
    fixed = [other]
    fixed += [x_peer(k)[1] for k in range(1, 4)]
    fixed += [y_peer(k)[1] for k in range(1, 4)]
    fixed += [z_peer(k)[1] for k in range(1, 8)]
    for q in range(4):

        @pl.when(has[q])
        def _():
            pl.semaphore_signal(barrier, inc=1, device_id=nxt[q], device_id_type=MESH)

    for peer in fixed:
        pl.semaphore_signal(barrier, inc=1, device_id=peer, device_id_type=MESH)

    loads[0].wait()
    for q in range(4):
        for s in range(2):
            pack[q, s] = loc[list_s[0, 0, s, q]]

    peers = len(fixed)
    for flag in has:
        peers += jnp.where(flag, 1, 0)
    pl.semaphore_wait(barrier, peers)

    def remote(src, dst, send, recv, to):
        return pltpu.make_async_remote_copy(
            src_ref=src, dst_ref=dst, send_sem=send, recv_sem=recv,
            device_id=to, device_id_type=MESH,
        )

    halo = [
        remote(pack.at[q], ext.at[pl.ds(2 + 2 * q, 2)], hs_sem.at[q], hr_sem.at[q], nxt[q])
        for q in range(4)
    ]
    for q in range(4):

        @pl.when(has[q])
        def _():
            halo[q].start()

    loads[1].wait()
    loads[2].wait()
    lane = lax.broadcasted_iota(jnp.int32, (Q, Q), 0)

    def before(i, c):
        rows = pl.ds(i * H, H)
        for u in range(2):
            t = 2 * i + u
            hot = picked(lane == perm_ref[0, t])
            pt[t] = hot.astype(BF16)
            pm[t] = hot.T.astype(BF16)
            hr[pl.ds(t * Q, Q), :] = loc[recv_s[0, 0, t]]
        aff[rows, :] = (
            dot(edges[rows, :], ew1[pl.ds(0, D), :])
            + dot(hr[rows, :], ew1[pl.ds(D, D), :])
            + eb1[...]
        )
        return c

    lax.fori_loop(0, 3, before, 0)
    agg[...] = jnp.zeros_like(agg)
    for load in loads[3:]:
        load.wait()
    came = (gx > 0, gx < 31, gy > 0, gy < 7)
    for q in range(4):

        @pl.when(came[q])
        def _():
            halo[q].wait_recv()

    def forward(i, c):
        rows = pl.ds(i * H, H)
        for u in range(2):
            t = 2 * i + u
            hs[pl.ds(t * Q, Q), :] = dot(pm[t], ext[send_s[0, 0, t]]).astype(BF16)
        hidden, slope = silu_parts(aff[rows, :] + dot(hs[rows, :], ew1[pl.ds(2 * D, D), :]))
        hid[rows, :] = hidden
        aff[rows, :] = slope
        message, inv = normed_rows(dot(hidden, ew2[...]))
        msg[rows, :] = message
        einv[rows, :] = inv
        for b in range(2):
            agg[b] += message[:Q] * picked(recv_s[0, 0, 2 * i] == b) + message[Q:] * picked(
                recv_s[0, 0, 2 * i + 1] == b
            )
        return c

    lax.fori_loop(0, 3, forward, 0)

    mine_cols = pl.ds(pl.multiple_of(core * H, H), H)
    their_cols = pl.ds(pl.multiple_of((1 - core) * H, H), H)
    for b in range(2):
        nin[pl.ds(b * Q, Q), pl.ds(0, D)] = loc[b]
        nin[pl.ds(b * Q, Q), pl.ds(D, D)] = agg[b].astype(BF16)
    nhid, nslope = silu_parts(dot(nin[...], nw1[...]) + nb1[...])
    nmsg, ninv = normed_rows(dot(nhid, nw2[...]))
    nout[...] = (nin[:, :D].astype(F32) + nmsg).astype(BF16)
    out_node = pltpu.make_async_copy(nout, nout_h, out_sem.at[0])
    out_node.start()
    gnl = norm_back(nmsg, ninv, cotn[...].astype(F32)).astype(BF16)
    gel_p[pl.ds(0, H), :] = gnl
    gnl_p[:, pl.ds(0, H)] = gel_p[pl.ds(0, H), their_cols]
    gnl_p[:, pl.ds(H, H)] = gel_p[pl.ds(0, H), mine_cols]
    gna = (dot_t(gnl, nw2[...]) * nslope).astype(BF16)
    gel_p[pl.ds(0, H), :] = gna
    gna_p[:, pl.ds(0, H)] = gel_p[pl.ds(0, H), their_cols]
    gna_p[:, pl.ds(H, H)] = gel_p[pl.ds(0, H), mine_cols]
    ginput = dot_t(gna, nw1[...])
    for b in range(2):
        owned[b] = ginput[b * Q : (b + 1) * Q, :D]
        gagg[b] = ginput[b * Q : (b + 1) * Q, D:]

    cores = [
        remote(
            gsend.at[pl.ds(lo, n), :], grecv.at[pl.ds(lo, n), :],
            cs_sem.at[i], cr_sem.at[i], other,
        )
        for i, (lo, n) in enumerate(PIECES)
    ]

    def put(at, value):
        gsend[pl.ds(at, H), :] = value[:, :H].astype(BF16)
        gown[pl.ds(at, H), :] = value[:, H:]

    def outer(left, right, base, blocks):
        def one(j, c):
            j = pl.multiple_of(j * H, H)
            put(base + j, t_dot(left[:, pl.ds(j, H)], right[...]))
            return c

        lax.fori_loop(0, blocks, one, 0)

    geap[pl.ds(0, H), :] = nhid
    outer_rows = geap.at[pl.ds(0, H), :]
    outer(outer_rows, gnl_p, 6 * D, 2)
    outer(nin, gna_p, 4 * D, 4)
    cores[0].start()

    def backward(i, c):
        rows = pl.ds(i * H, H)
        up = jnp.concatenate(
            [gagg[recv_s[0, 0, 2 * i]], gagg[recv_s[0, 0, 2 * i + 1]]], axis=0
        ) + cote[rows, :].astype(F32)
        gel = norm_back(msg[rows, :], einv[rows, :], up).astype(BF16)
        gea[rows, :] = gel
        gel_p[rows, pl.ds(0, H)] = gea[rows, their_cols]
        gel_p[rows, pl.ds(H, H)] = gea[rows, mine_cols]
        gea[rows, :] = (dot_t(gel, ew2[...]) * aff[rows, :]).astype(BF16)
        geap[rows, pl.ds(0, H)] = gea[rows, their_cols]
        geap[rows, pl.ds(H, H)] = gea[rows, mine_cols]
        return c

    lax.fori_loop(0, 3, backward, 0)
    outer(hid, gel_p, 3 * D, 2)
    cores[1].start()

    def pair_sum(lo, hi):
        def one(j, c):
            rows = pl.ds(pl.multiple_of(j * BLK, 16), BLK)
            total = (gown[rows, :] + grecv[rows, :].astype(F32)).astype(BF16)
            g1a[j // 4, j % 4] = total[:, :Q]
            g1b[j // 4, (j // 4 + j) % 4] = total[:, Q:]
            return c

        lax.fori_loop(lo, hi, one, 0)

    early, late = [], []
    for got, lo, n, sem in ((early, EARLY, NGROUP - EARLY, 0), (late, 0, EARLY, 3)):
        for k in range(1, 4):
            to, who = x_peer(k)
            got.append(
                remote(
                    g1a.at[pl.ds(lo, n), to], r1a.at[k - 1, pl.ds(lo, n)],
                    as_sem.at[sem + k - 1], ar_sem.at[sem + k - 1], who,
                )
            )
            to, who = y_peer(k)
            got.append(
                remote(
                    g1b.at[pl.ds(lo, n), to], r1b.at[k - 1, pl.ds(lo, n)],
                    ys_sem.at[sem + k - 1], yr_sem.at[sem + k - 1], who,
                )
            )

    cores[0].wait_recv()
    pair_sum(4 * EARLY, 32)
    for copy in early:
        copy.start()

    outer(edges, geap, 0, 2)
    cores[2].start()
    outer(hr, geap, D, 2)
    cores[3].start()
    outer(hs, geap, 2 * D, 2)
    cores[4].start()
    for copy in cores[1:]:
        copy.wait_recv()
    pair_sum(0, 4 * EARLY)
    for copy in late:
        copy.start()

    def inputs(i, c):
        rows = pl.ds(i * H, H)
        part = gea[rows, :]
        egrad[rows, :] = (
            cote[rows, :].astype(F32) + dot_t(part, ew1[pl.ds(0, D), :])
        ).astype(BF16)
        grad_r = dot_t(part, ew1[pl.ds(D, D), :])
        for b in range(2):
            owned[b] += grad_r[:Q] * picked(recv_s[0, 0, 2 * i] == b) + grad_r[Q:] * picked(
                recv_s[0, 0, 2 * i + 1] == b
            )
        for u in range(2):
            t = 2 * i + u
            rows_t = pl.ds(t * Q, Q)
            hs[rows_t, :] = dot(pt[t], gea[rows_t, :]).astype(BF16)
        grad_s = dot_t(hs[rows, :], ew1[pl.ds(2 * D, D), :])
        for u in range(2):
            xs[2 * i + u] = grad_s[u * Q : (u + 1) * Q]
        return c

    lax.fori_loop(0, 3, inputs, 0)
    out_edge = pltpu.make_async_copy(egrad, egrad_h, out_sem.at[1])
    out_edge.start()

    def slots(b, c):
        total = xs[0] * picked(send_s[0, 0, 0] == b + 2)
        for t in range(1, 6):
            total += xs[t] * picked(send_s[0, 0, t] == b + 2)
        hret[b // 2, b % 2] = total.astype(BF16)
        return c

    lax.fori_loop(0, 8, slots, 0)
    back = (nxt[1], nxt[0], nxt[3], nxt[2])
    home = [
        remote(hret.at[q], ret.at[q], bs_sem.at[q], br_sem.at[q], back[q]) for q in range(4)
    ]
    for q in range(4):

        @pl.when(came[q])
        def _():
            home[q].start()

    for b in range(2):
        total = owned[b] + cotn[pl.ds(b * Q, Q), :].astype(F32)
        for t in range(6):
            total += xs[t] * picked(send_s[0, 0, t] == b)
        owned[b] = total

    def sum_first(g, c):
        total = g1a[g, x].astype(F32)
        for k in range(3):
            total += r1a[k, g].astype(F32)
        g2a[(g + x) % 4, g // 4] = total.astype(BF16)
        total = g1b[g, y].astype(F32)
        for k in range(3):
            total += r1b[k, g].astype(F32)
        g2b[(y + 8 - g) % 4, g // 4] = total.astype(BF16)
        return c

    for copy in early:
        copy.wait_recv()
    lax.fori_loop(EARLY, NGROUP, sum_first, 0)
    for copy in late:
        copy.wait_recv()
    lax.fori_loop(0, EARLY, sum_first, 0)
    second = []
    for k in range(1, 4):
        to, who = y_peer(k)
        second.append(
            remote(g2a.at[to], r2a.at[k - 1], a2s_sem.at[k - 1], a2r_sem.at[k - 1], who)
        )
        to, who = x_peer(k)
        second.append(
            remote(g2b.at[to], r2b.at[k - 1], b2s_sem.at[k - 1], b2r_sem.at[k - 1], who)
        )
    for copy in second:
        copy.start()

    for copy in second:
        copy.wait_recv()
    for g in range(2):
        total = g2a[y, g].astype(F32)
        for k in range(3):
            total += r2a[k, g].astype(F32)
        g3[g, pl.ds(0, BLK), pl.ds(0, Q)] = total
        total = g2b[x, g].astype(F32)
        for k in range(3):
            total += r2b[k, g].astype(F32)
        g3[g, pl.ds(0, BLK), pl.ds(Q, Q)] = total
        g3[g, pl.ds(BLK, 16), :] = jnp.zeros((16, H), F32)
        for h in range(4):
            s3[4 * g + h] = g3[g, pl.ds(CHIP_ROWS * h, 32), :].astype(BF16)
    along = []
    for k in range(1, 8):
        to, who = z_peer(k)
        along.append(
            remote(s3.at[to], r3.at[k - 1], zs_sem.at[k - 1], zr_sem.at[k - 1], who)
        )
    for copy in along:
        copy.start()

    for q in range(4):

        @pl.when(has[q])
        def _():
            halo[q].wait_send()

    for copy in cores + early + late + second:
        copy.wait_send()
    for copy in along:
        copy.wait_recv()
    total = s3[z_lo * 4 + z_hi].astype(F32)
    for k in range(7):
        total += r3[k].astype(F32)
    fin[...] = total

    def node_gradient():
        for q in range(4):

            @pl.when(has[q])
            def _():
                home[q].wait_recv()

        for b in range(2):
            total = owned[b]
            for q in range(4):
                for s in range(2):
                    wanted = jnp.logical_and(list_s[0, 0, s, q] == b, count_s[0, 0, q] > s)
                    weight = jnp.where(wanted, 1, 0) * jnp.ones((Q, D), jnp.int32)
                    total += jnp.where(weight > 0, ret[q, s].astype(F32), 0.0)
            ngrad[pl.ds(b * Q, Q), :] = total.astype(BF16)
        out_grad = pltpu.make_async_copy(ngrad, ngrad_h, out_sem.at[2])
        out_grad.start()
        return out_grad

    swap_s[0] = fin[pl.ds(0, 16), :]
    swap_s[1] = fin[pl.ds(14, 16), :]
    swap = [
        remote(swap_s.at[c], swap_r.at[core], ws_sem.at[c], wr_sem.at[core], (own_blk, z_hi * 2 + c))
        for c in range(2)
    ]
    stay = pltpu.make_async_copy(swap_s.at[core], swap_r.at[core], in_sem.at[0])
    for c in range(2):

        @pl.when(jnp.logical_or(own_blk != gx, core != c))
        def _():
            swap[c].start()

    @pl.when(own_blk == gx)
    def _():
        stay.start()

    local = lax.broadcasted_iota(jnp.int32, (32, H), 0)
    row = local + CHIP_ROWS * (own_blk * 4 + z_hi)
    square = jnp.where(local < CHIP_ROWS, total * total, 0.0)
    square = square[:, :Q] + square[:, Q:]
    row = row[:, :Q]
    cuts = (0,) + BOUNDS + (ROWS,)
    pieces = [
        jnp.sum(
            jnp.where(jnp.logical_and(row >= cuts[m], row < cuts[m + 1]), square, 0.0),
            axis=0, keepdims=True,
        )
        for m in range(4)
    ]
    stat = jnp.concatenate(pieces + [jnp.zeros((4, Q), F32)], axis=0)
    rounds = ([], [])
    for k in range(1, 16):
        to = (z + k % 8) % 8
        rounds[0].append((y * 8 + (to % 2) * 4 + x, (to // 2) * 2 + (core + k // 8) % 2))
        rounds[1].append((((y + k // 4) % 4) * 8 + z_lo * 4 + (x + k % 4) % 4, gy))
    stat_copies = []
    for r, peers in enumerate(rounds):
        stat_s[r] = stat
        for i, who in enumerate(peers):
            remote(stat_s.at[r], stat_r.at[r, i], ts_sem.at[r], tr_sem.at[r], who).start()
        everyone = remote(stat_r.at[r], stat_r.at[r], ts_sem.at[r], tr_sem.at[r], peers[0])
        if r == 1:
            out_grad = node_gradient()
        everyone.wait_recv()
        for i in range(15):
            stat = stat + stat_r[r, i]
        stat_copies.append(everyone)

    taken = [
        remote(swap_s.at[c], swap_r.at[c], ws_sem.at[c], wr_sem.at[c], (from_gx, z_hi * 2 + c))
        for c in range(2)
    ]
    for c in range(2):

        @pl.when(jnp.logical_or(from_gx != gx, core != c))
        def _():
            taken[c].wait_recv()

    @pl.when(own_blk == gx)
    def _():
        stay.wait()

    scales = [
        lax.rsqrt(jnp.sum(stat[m : m + 1], axis=-1, keepdims=True) * (1.0 / SIZES[m]) + 1e-06)
        for m in range(4)
    ]
    row = lax.broadcasted_iota(jnp.int32, (16, H), 0) + 14 * (gx * 8 + gy)
    scale = jnp.where(
        row < BOUNDS[0],
        scales[0],
        jnp.where(row < BOUNDS[1], scales[1], jnp.where(row < BOUNDS[2], scales[2], scales[3])),
    )
    left = swap_r[0] * scale
    right = swap_r[1] * scale
    for g in range(2):
        flat[pl.ds(g, 16, stride=4), :] = left[:, g * Q : (g + 1) * Q]
        flat[pl.ds(2 + g, 16, stride=4), :] = right[:, g * Q : (g + 1) * Q]
    wdir[...] = flat[pl.ds(0, 56), :].astype(BF16)

    for q in range(4):

        @pl.when(came[q])
        def _():
            home[q].wait_send()

    for copy in along + stat_copies:
        copy.wait_send()
    for c in range(2):

        @pl.when(jnp.logical_or(own_blk != gx, core != c))
        def _():
            swap[c].wait_send()

    out_node.wait()
    out_edge.wait()
    out_grad.wait()


def hand_over(*refs):
    given, results, held, sem_in, sem_out = refs[:4], refs[4:8], refs[8:12], refs[12], refs[13]
    into = [pltpu.make_async_copy(given[i], held[i], sem_in.at[i]) for i in range(4)]
    out = [pltpu.make_async_copy(held[i], results[i], sem_out.at[i]) for i in range(4)]
    for copy in into:
        copy.start()
    for i in range(4):
        into[i].wait()
        out[i].start()
    for copy in out:
        copy.wait()


def on_device(
    node_latents, edge_latents, edge_w1, edge_b1, edge_w2, node_w1, node_b1, node_w2,
    node_cot, edge_cot, send_count, send_list, tile_recv, tile_send, tile_perm,
):
    hbm = pl.BlockSpec(memory_space=pl.ANY)
    vmem = pl.BlockSpec(memory_space=pltpu.VMEM)
    smem = pl.BlockSpec(memory_space=pltpu.SMEM)
    b = functools.partial(pltpu.VMEM, dtype=BF16)
    f = functools.partial(pltpu.VMEM, dtype=F32)
    sem = lambda n: pltpu.SemaphoreType.DMA((n,))
    scratch = [
        b((2, Q, D)), b((10, Q, D)), b((768, D)), b((3 * D, D)), b((D, D)), b((2 * D, D)), b((D, D)),
        b((H, D)), b((768, D)), b((4, 2, Q, D)), b((6, Q, Q)), b((6, Q, Q)),
        b((768, D)), b((768, D)), f((768, D)), b((768, D)), f((768, D)), f((768, 1)),
        f((2, Q, D)), f((2, Q, D)), f((2, Q, D)), b((768, D)), b((768, D)), b((768, D)),
        b((H, 2 * D)), b((H, D)), b((H, D)), f((6, Q, D)), b((4, 2, Q, D)), b((4, 2, Q, D)),
        b((H, D)), b((H, D)), b((768, D)),
        b((ROWS, H)), f((ROWS, H)), b((ROWS, H)),
        b((8, 4, BLK, Q)), b((8, 4, BLK, Q)), b((3, 8, BLK, Q)), b((3, 8, BLK, Q)),
        b((4, 2, BLK, Q)), b((4, 2, BLK, Q)), b((3, 2, BLK, Q)), b((3, 2, BLK, Q)),
        f((2, Q, H)), b((8, 32, H)), b((7, 32, H)), f((32, H)), f((2, 16, H)), f((2, 16, H)),
        f((2, 8, Q)), f((2, 15, 8, Q)), f((64, Q)),
        sem(9), sem(3), sem(4), sem(4), sem(4), sem(4), sem(5), sem(5),
        sem(6), sem(6), sem(6), sem(6), sem(3), sem(3), sem(3), sem(3),
        sem(7), sem(7), sem(2), sem(2), sem(2), sem(2),
    ]
    shapes = (
        jax.ShapeDtypeStruct((H, D), BF16),
        jax.ShapeDtypeStruct((H, D), BF16),
        jax.ShapeDtypeStruct((768, D), BF16),
        jax.ShapeDtypeStruct((56, Q), BF16),
    )
    results = pl.pallas_call(
        kernel,
        out_shape=shapes,
        in_specs=[smem] * 4 + [vmem] * 3 + [hbm] * 8,
        out_specs=(hbm, hbm, hbm, vmem),
        scratch_shapes=scratch,
        compiler_params=pltpu.CompilerParams(
            collective_id=0, has_side_effects=True, vmem_limit_bytes=56 * 1024 * 1024
        ),
        name="layer",
    )(
        send_count, jnp.transpose(send_list, (0, 1, 3, 2)), tile_recv, tile_send,
        jnp.transpose(tile_perm, (0, 2, 1, 3)),
        edge_b1.reshape(1, D), node_b1.reshape(1, D),
        node_latents.reshape(2, Q, D), edge_latents.reshape(768, D),
        edge_w1, edge_w2, node_w1, node_w2,
        node_cot.reshape(H, D), edge_cot.reshape(768, D),
    )
    nout, ngrad, egrad, wdir = pl.pallas_call(
        hand_over,
        out_shape=shapes,
        in_specs=[hbm] * 4,
        out_specs=(hbm,) * 4,
        scratch_shapes=[b((H, D)), b((H, D)), b((768, D)), b((56, Q)), sem(4), sem(4)],
        name="hand_over",
    )(*results)
    return (
        nout.reshape(1, 1, H, D),
        ngrad.reshape(1, 1, H, D),
        egrad.reshape(1, 1, 768, D),
        wdir.reshape(7168),
    )


def solution(mesh):
    cells = P("gx", "gy", None, None)
    flat = P("gx", "gy", None)
    return jax.shard_map(
        on_device,
        mesh=mesh,
        in_specs=(
            cells, cells, P(), P(), P(), P(), P(), P(), cells, cells,
            flat, cells, flat, flat, cells,
        ),
        out_specs=(cells, cells, cells, P(("gx", "gy"))),
        check_vma=False,
    )
```

```python
import functools

import jax
import jax.numpy as jnp
from jax import lax
from jax.experimental import pallas as pl
from jax.experimental.pallas import tpu as pltpu
from jax.sharding import PartitionSpec as P

MESH = pl.DeviceIdType.MESH
F32 = jnp.float32
BF16 = jnp.bfloat16
D = 512
H = 256
Q = 128
ROWS = 7 * D
CHIP_ROWS = 28
BLK = 112
PARTS = ((4, 8), (0, 2), (2, 4))
BOUNDS = (3 * D, 4 * D, 6 * D)
SIZES = (3 * D * D, D * D, 2 * D * D, D * D)
PIECES = ((4 * D, 3 * D), (3 * D, D), (0, D), (D, D), (2 * D, D))


def dot(a, b):
    return jnp.dot(a, b, preferred_element_type=F32)


def dot_t(a, b):
    return lax.dot_general(a, b, (((1,), (1,)), ((), ())), preferred_element_type=F32)


def t_dot(a, b):
    return lax.dot_general(a, b, (((0,), (0,)), ((), ())), preferred_element_type=F32)


def normed_rows(values):
    center = values - jnp.mean(values, axis=-1, keepdims=True)
    inv = lax.rsqrt(jnp.mean(center * center, axis=-1, keepdims=True) + 1e-05)
    return center * inv, inv


def norm_back(normed, inv, up):
    return inv * (
        up
        - jnp.mean(up, axis=-1, keepdims=True)
        - normed * jnp.mean(up * normed, axis=-1, keepdims=True)
    )


def silu_parts(v):
    s = jax.nn.sigmoid(v)
    return (v * s).astype(BF16), s * (1.0 + v * (1.0 - s))


def picked(flag):
    return jnp.where(flag, 1.0, 0.0).astype(F32)


def kernel(
    count_s, list_s, recv_s, send_s, perm_ref, eb1, nb1,
    nodes_h, edges_h, ew1_h, ew2_h, nw1_h, nw2_h, cotn_h, cote_h,
    nout_h, ngrad_h, egrad_h, wdir,
    loc, ext, edges, ew1, ew2, nw1, nw2, cotn, cote, pack, pt, pm,
    edges_t, hr_t, loc_t, hr, hs, aff, hid, msg, einv, agg, gagg, owned, gea, geap, gel_p,
    nin, gna_p, gnl_p, xs, hret, ret, nout, ngrad, egrad,
    gsend, gown, grecv, g1a, g1b, r1a, r1b, via_a, via_b, g2a, g2b, r2a, r2b,
    g3, s3, r3, fin, swap_s, swap_r, stat_s, stat_r, flat,
    in_sem, out_sem, hs_sem, hr_sem, bs_sem, br_sem, cs_sem, cr_sem,
    ms_sem, mr_sem, ns_sem, nr_sem, as_sem, ar_sem, ys_sem, yr_sem, a2s_sem, a2r_sem, b2s_sem, b2r_sem,
    zs_sem, zr_sem, ws_sem, wr_sem, ts_sem, tr_sem,
):
    gx = lax.axis_index("gx")
    gy = lax.axis_index("gy")
    y = gx // 8
    z_lo = (gx // 4) % 2
    x = gx % 4
    z_hi = gy // 2
    core = gy % 2
    z = z_hi * 2 + z_lo
    other = (gx, z_hi * 2 + (1 - core))

    def x_peer(k):
        to = (x + k) % 4
        return to, (y * 8 + z_lo * 4 + to, gy)

    def y_peer(k):
        to = (y + k) % 4
        return to, (to * 8 + z_lo * 4 + x, gy)

    def z_peer(k):
        to = (z + k) % 8
        lo, hi = to % 2, to // 2
        return lo * 4 + hi, (y * 8 + lo * 4 + x, hi * 2 + core)

    own_blk = z_lo * 16 + ((y + 4 - x) % 4) * 4 + x
    from_gx = ((gx // 4 + x) % 4) * 8 + (gx // 16) * 4 + x

    nxt = ((gx + 1, gy), (gx - 1, gy), (gx, gy + 1), (gx, gy - 1))
    has = (gx < 31, gx > 0, gy < 7, gy > 0)

    loads = [
        pltpu.make_async_copy(src, dst, in_sem.at[i])
        for i, (src, dst) in enumerate(
            (
                (nodes_h, loc),
                (edges_h, edges),
                (ew1_h, ew1),
                (ew2_h, ew2),
                (nw1_h, nw1),
                (nw2_h, nw2),
                (cotn_h, cotn),
                (cote_h, cote),
                (nodes_h, ext.at[pl.ds(0, 2)]),
            )
        )
    ]
    loads[0].start()
    barrier = pltpu.get_barrier_semaphore()
    fixed = [other]
    fixed += [x_peer(k)[1] for k in range(1, 4)]
    fixed += [y_peer(k)[1] for k in range(1, 4)]
    fixed += [z_peer(k)[1] for k in range(1, 8)]
    for peer in reversed(fixed):
        pl.semaphore_signal(barrier, inc=1, device_id=peer, device_id_type=MESH)

    for q in range(4):

        @pl.when(has[q])
        def _():
            pl.semaphore_signal(barrier, inc=1, device_id=nxt[q], device_id_type=MESH)

    for load in loads[1:]:
        load.start()

    loads[0].wait()
    for q in range(4):
        for s in range(2):
            pack[q, s] = loc[list_s[0, 0, s, q]]

    peers = len(fixed)
    for flag in has:
        peers += jnp.where(flag, 1, 0)
    pl.semaphore_wait(barrier, peers)

    def remote(src, dst, send, recv, to):
        return pltpu.make_async_remote_copy(
            src_ref=src, dst_ref=dst, send_sem=send, recv_sem=recv,
            device_id=to, device_id_type=MESH,
        )

    halo = [
        remote(pack.at[q], ext.at[pl.ds(2 + 2 * q, 2)], hs_sem.at[q], hr_sem.at[q], nxt[q])
        for q in range(4)
    ]
    for q in range(4):

        @pl.when(has[q])
        def _():
            halo[q].start()

    loads[1].wait()
    loads[2].wait()
    lane = lax.broadcasted_iota(jnp.int32, (Q, Q), 0)

    def before(i, c):
        rows = pl.ds(i * H, H)
        for u in range(2):
            t = 2 * i + u
            hot = picked(lane == perm_ref[0, t])
            pt[t] = hot.astype(BF16)
            pm[t] = hot.T.astype(BF16)
            hr[pl.ds(t * Q, Q), :] = loc[recv_s[0, 0, t]]
        aff[rows, :] = (
            dot(edges[rows, :], ew1[pl.ds(0, D), :])
            + dot(hr[rows, :], ew1[pl.ds(D, D), :])
            + eb1[...]
        )
        return c

    lax.fori_loop(0, 3, before, 0)

    def turn(i, c):
        rows = pl.ds(pl.multiple_of(i * H, H), H)
        edges_t[:, rows] = edges[rows, :].T
        hr_t[:, rows] = hr[rows, :].T
        return c

    lax.fori_loop(0, 3, turn, 0)
    for b in range(2):
        loc_t[:, pl.ds(b * Q, Q)] = loc[b].T
    agg[...] = jnp.zeros_like(agg)
    for load in loads[3:]:
        load.wait()
    came = (gx > 0, gx < 31, gy > 0, gy < 7)
    for q in range(4):

        @pl.when(came[q])
        def _():
            halo[q].wait_recv()

    def forward(i, c):
        rows = pl.ds(i * H, H)
        for u in range(2):
            t = 2 * i + u
            hs[pl.ds(t * Q, Q), :] = dot(pm[t], ext[send_s[0, 0, t]]).astype(BF16)
        hidden, slope = silu_parts(aff[rows, :] + dot(hs[rows, :], ew1[pl.ds(2 * D, D), :]))
        hid[rows, :] = hidden
        aff[rows, :] = slope
        message, inv = normed_rows(dot(hidden, ew2[...]))
        msg[rows, :] = message
        einv[rows, :] = inv
        for b in range(2):
            agg[b] += message[:Q] * picked(recv_s[0, 0, 2 * i] == b) + message[Q:] * picked(
                recv_s[0, 0, 2 * i + 1] == b
            )
        return c

    lax.fori_loop(0, 3, forward, 0)

    mine_cols = pl.ds(pl.multiple_of(core * H, H), H)
    their_cols = pl.ds(pl.multiple_of((1 - core) * H, H), H)
    for b in range(2):
        nin[pl.ds(b * Q, Q), pl.ds(0, D)] = loc[b]
        nin[pl.ds(b * Q, Q), pl.ds(D, D)] = agg[b].astype(BF16)
    nhid, nslope = silu_parts(dot(nin[...], nw1[...]) + nb1[...])
    nmsg, ninv = normed_rows(dot(nhid, nw2[...]))
    nout[...] = (nin[:, :D].astype(F32) + nmsg).astype(BF16)
    out_node = pltpu.make_async_copy(nout, nout_h, out_sem.at[0])
    out_node.start()
    gnl = norm_back(nmsg, ninv, cotn[...].astype(F32)).astype(BF16)
    gel_p[pl.ds(0, H), :] = gnl
    gnl_p[:, pl.ds(0, H)] = gel_p[pl.ds(0, H), their_cols]
    gnl_p[:, pl.ds(H, H)] = gel_p[pl.ds(0, H), mine_cols]
    gna = (dot_t(gnl, nw2[...]) * nslope).astype(BF16)
    gel_p[pl.ds(0, H), :] = gna
    gna_p[:, pl.ds(0, H)] = gel_p[pl.ds(0, H), their_cols]
    gna_p[:, pl.ds(H, H)] = gel_p[pl.ds(0, H), mine_cols]
    ginput = dot_t(gna, nw1[...])
    for b in range(2):
        owned[b] = ginput[b * Q : (b + 1) * Q, :D]
        gagg[b] = ginput[b * Q : (b + 1) * Q, D:]

    cores = [
        remote(
            gsend.at[pl.ds(lo, n), :], grecv.at[pl.ds(lo, n), :],
            cs_sem.at[i], cr_sem.at[i], other,
        )
        for i, (lo, n) in enumerate(PIECES)
    ]

    def put(at, value):
        gsend[pl.ds(at, H), :] = value[:, :H].astype(BF16)
        gown[pl.ds(at, H), :] = value[:, H:]

    def outer(left, right, base, blocks):
        def one(j, c):
            j = pl.multiple_of(j * H, H)
            put(base + j, t_dot(left[:, pl.ds(j, H)], right[...]))
            return c

        lax.fori_loop(0, blocks, one, 0)

    def outer_turned(left, right, base, blocks):
        def one(j, c):
            j = pl.multiple_of(j * H, H)
            put(base + j, dot(left[pl.ds(j, H), :], right[...]))
            return c

        lax.fori_loop(0, blocks, one, 0)

    geap[pl.ds(0, H), :] = nhid
    outer_rows = geap.at[pl.ds(0, H), :]
    outer(outer_rows, gnl_p, 6 * D, 2)
    outer_turned(loc_t, gna_p, 4 * D, 2)
    outer(nin.at[:, pl.ds(D, D)], gna_p, 5 * D, 2)
    cores[0].start()

    def backward(i, c):
        rows = pl.ds(i * H, H)
        up = jnp.concatenate(
            [gagg[recv_s[0, 0, 2 * i]], gagg[recv_s[0, 0, 2 * i + 1]]], axis=0
        ) + cote[rows, :].astype(F32)
        gel = norm_back(msg[rows, :], einv[rows, :], up).astype(BF16)
        gea[rows, :] = gel
        gel_p[rows, pl.ds(0, H)] = gea[rows, their_cols]
        gel_p[rows, pl.ds(H, H)] = gea[rows, mine_cols]
        gea[rows, :] = (dot_t(gel, ew2[...]) * aff[rows, :]).astype(BF16)
        geap[rows, pl.ds(0, H)] = gea[rows, their_cols]
        geap[rows, pl.ds(H, H)] = gea[rows, mine_cols]
        return c

    lax.fori_loop(0, 3, backward, 0)
    outer(hid, gel_p, 3 * D, 2)
    cores[1].start()

    def pair_sum(lo, hi):
        def one(j, c):
            rows = pl.ds(pl.multiple_of(j * BLK, 16), BLK)
            total = (gown[rows, :] + grecv[rows, :].astype(F32)).astype(BF16)
            g1a[j // 4, j % 4] = total[:, :Q]
            g1b[j // 4, (j // 4 + j) % 4] = total[:, Q:]
            return c

        lax.fori_loop(lo, hi, one, 0)

    ahead, right = x_peer(1)
    behind, left = x_peer(3)
    above, upper = y_peer(1)
    below, lower = y_peer(3)
    x_far, y_far = (x + 2) % 4, (y + 2) % 4
    through, first = [], []
    for p, (lo, hi) in enumerate(PARTS):
        n = (hi - lo) // 2
        one, two, i = pl.ds(lo, n), pl.ds(lo + n, n), 2 * p
        through.append(
            [
                remote(g1a.at[one, x_far], via_a.at[one], ms_sem.at[i], mr_sem.at[i], right),
                remote(g1b.at[one, y_far], via_b.at[one], ns_sem.at[i], nr_sem.at[i], upper),
                remote(g1a.at[two, x_far], via_a.at[two], ms_sem.at[i + 1], mr_sem.at[i + 1], left),
                remote(g1b.at[two, y_far], via_b.at[two], ns_sem.at[i + 1], nr_sem.at[i + 1], lower),
            ]
        )
        both = pl.ds(lo, hi - lo)
        first.append(
            [
                remote(g1a.at[both, ahead], r1a.at[0, both], as_sem.at[i], ar_sem.at[i], right),
                remote(g1b.at[both, above], r1b.at[0, both], ys_sem.at[i], yr_sem.at[i], upper),
                remote(g1a.at[both, behind], r1a.at[1, both], as_sem.at[i + 1], ar_sem.at[i + 1], left),
                remote(g1b.at[both, below], r1b.at[1, both], ys_sem.at[i + 1], yr_sem.at[i + 1], lower),
            ]
        )

    def first_half(p, needed):
        for copy in needed:
            copy.wait_recv()
        pair_sum(4 * PARTS[p][0], 4 * PARTS[p][1])
        for copy in through[p]:
            copy.start()

    def second_half(p):
        lo, hi = PARTS[p]
        mid = (lo + hi) // 2
        for copy in through[p]:
            copy.wait_recv()

        def merge(x_to, y_to):
            def one(g, c):
                g1a[g, x_to] = (g1a[g, x_to].astype(F32) + via_a[g].astype(F32)).astype(BF16)
                g1b[g, y_to] = (g1b[g, y_to].astype(F32) + via_b[g].astype(F32)).astype(BF16)
                return c

            return one

        lax.fori_loop(lo, mid, merge(ahead, above), 0)
        lax.fori_loop(mid, hi, merge(behind, below), 0)
        for copy in first[p]:
            copy.start()

    outer_turned(edges_t, geap, 0, 2)
    cores[2].start()
    first_half(0, cores[:2])
    outer_turned(hr_t, geap, D, 2)
    cores[3].start()
    outer(hs, geap, 2 * D, 2)
    cores[4].start()
    second_half(0)
    first_half(1, cores[2:4])
    first_half(2, cores[4:])
    second_half(1)
    second_half(2)

    def inputs(i, c):
        rows = pl.ds(i * H, H)
        part = gea[rows, :]
        egrad[rows, :] = (
            cote[rows, :].astype(F32) + dot_t(part, ew1[pl.ds(0, D), :])
        ).astype(BF16)
        grad_r = dot_t(part, ew1[pl.ds(D, D), :])
        for b in range(2):
            owned[b] += grad_r[:Q] * picked(recv_s[0, 0, 2 * i] == b) + grad_r[Q:] * picked(
                recv_s[0, 0, 2 * i + 1] == b
            )
        for u in range(2):
            t = 2 * i + u
            rows_t = pl.ds(t * Q, Q)
            hs[rows_t, :] = dot(pt[t], gea[rows_t, :]).astype(BF16)
        grad_s = dot_t(hs[rows, :], ew1[pl.ds(2 * D, D), :])
        for u in range(2):
            xs[2 * i + u] = grad_s[u * Q : (u + 1) * Q]
        return c

    lax.fori_loop(0, 3, inputs, 0)
    out_edge = pltpu.make_async_copy(egrad, egrad_h, out_sem.at[1])
    out_edge.start()

    def slots(b, c):
        total = xs[0] * picked(send_s[0, 0, 0] == b + 2)
        for t in range(1, 6):
            total += xs[t] * picked(send_s[0, 0, t] == b + 2)
        hret[b // 2, b % 2] = total.astype(BF16)
        return c

    lax.fori_loop(0, 8, slots, 0)
    back = (nxt[1], nxt[0], nxt[3], nxt[2])
    home = [
        remote(hret.at[q], ret.at[q], bs_sem.at[q], br_sem.at[q], back[q]) for q in range(4)
    ]
    for q in range(2, 4):

        @pl.when(came[q])
        def _():
            home[q].start()

    for b in range(2):
        total = owned[b] + cotn[pl.ds(b * Q, Q), :].astype(F32)
        for t in range(6):
            total += xs[t] * picked(send_s[0, 0, t] == b)
        owned[b] = total

    def sum_first(g, c):
        total = g1a[g, x].astype(F32)
        for k in range(2):
            total += r1a[k, g].astype(F32)
        g2a[(g + x) % 4, g // 4] = total.astype(BF16)
        total = g1b[g, y].astype(F32)
        for k in range(2):
            total += r1b[k, g].astype(F32)
        g2b[(y + 8 - g) % 4, g // 4] = total.astype(BF16)
        return c

    for p, (lo, hi) in enumerate(PARTS):
        for copy in first[p]:
            copy.wait_recv()
        lax.fori_loop(lo, hi, sum_first, 0)
    second = []
    for k in range(1, 4):
        to, who = y_peer(k)
        second.append(
            remote(g2a.at[to], r2a.at[k - 1], a2s_sem.at[k - 1], a2r_sem.at[k - 1], who)
        )
        to, who = x_peer(k)
        second.append(
            remote(g2b.at[to], r2b.at[k - 1], b2s_sem.at[k - 1], b2r_sem.at[k - 1], who)
        )
    for copy in second:
        copy.start()

    for copy in second:
        copy.wait_recv()
    for g in range(2):
        total = g2a[y, g].astype(F32)
        for k in range(3):
            total += r2a[k, g].astype(F32)
        g3[g, pl.ds(0, BLK), pl.ds(0, Q)] = total
        total = g2b[x, g].astype(F32)
        for k in range(3):
            total += r2b[k, g].astype(F32)
        g3[g, pl.ds(0, BLK), pl.ds(Q, Q)] = total
        g3[g, pl.ds(BLK, 16), :] = jnp.zeros((16, H), F32)
        for h in range(4):
            s3[4 * g + h] = g3[g, pl.ds(CHIP_ROWS * h, 32), :].astype(BF16)
    along = []
    for k in range(1, 8):
        to, who = z_peer(k)
        along.append(
            remote(s3.at[to], r3.at[k - 1], zs_sem.at[k - 1], zr_sem.at[k - 1], who)
        )
    for copy in along:
        copy.start()

    for q in range(2):

        @pl.when(came[q])
        def _():
            home[q].start()

    for q in range(4):

        @pl.when(has[q])
        def _():
            halo[q].wait_send()

    for copy in cores + through[0] + through[1] + through[2] + first[0] + first[1] + first[2] + second:
        copy.wait_send()
    for copy in along:
        copy.wait_recv()
    total = s3[z_lo * 4 + z_hi].astype(F32)
    for k in range(7):
        total += r3[k].astype(F32)
    fin[...] = total

    def node_gradient():
        for q in range(4):

            @pl.when(has[q])
            def _():
                home[q].wait_recv()

        for b in range(2):
            total = owned[b]
            for q in range(4):
                for s in range(2):
                    wanted = jnp.logical_and(list_s[0, 0, s, q] == b, count_s[0, 0, q] > s)
                    weight = jnp.where(wanted, 1, 0) * jnp.ones((Q, D), jnp.int32)
                    total += jnp.where(weight > 0, ret[q, s].astype(F32), 0.0)
            ngrad[pl.ds(b * Q, Q), :] = total.astype(BF16)
        out_grad = pltpu.make_async_copy(ngrad, ngrad_h, out_sem.at[2])
        out_grad.start()
        return out_grad

    swap_s[0] = fin[pl.ds(0, 16), :]
    swap_s[1] = fin[pl.ds(14, 16), :]
    swap = [
        remote(swap_s.at[c], swap_r.at[core], ws_sem.at[c], wr_sem.at[core], (own_blk, z_hi * 2 + c))
        for c in range(2)
    ]
    stay = pltpu.make_async_copy(swap_s.at[core], swap_r.at[core], in_sem.at[0])
    for c in range(2):

        @pl.when(jnp.logical_or(own_blk != gx, core != c))
        def _():
            swap[c].start()

    @pl.when(own_blk == gx)
    def _():
        stay.start()

    local = lax.broadcasted_iota(jnp.int32, (32, H), 0)
    row = local + CHIP_ROWS * (own_blk * 4 + z_hi)
    square = jnp.where(local < CHIP_ROWS, total * total, 0.0)
    square = square[:, :Q] + square[:, Q:]
    row = row[:, :Q]
    cuts = (0,) + BOUNDS + (ROWS,)
    pieces = [
        jnp.sum(
            jnp.where(jnp.logical_and(row >= cuts[m], row < cuts[m + 1]), square, 0.0),
            axis=0, keepdims=True,
        )
        for m in range(4)
    ]
    stat = jnp.concatenate(pieces + [jnp.zeros((4, Q), F32)], axis=0)
    rounds = (
        [other],
        [z_peer(k)[1] for k in range(1, 8)],
        [
            (((y + k // 4) % 4) * 8 + z_lo * 4 + (x + k % 4) % 4, gy)
            for k in (5, 7, 13, 15, 6, 9, 11, 14, 10, 1, 3, 4, 12, 2, 8)
        ],
    )
    stat_copies = []
    at = 0
    for r, peers in enumerate(rounds):
        n = len(peers)
        stat_s[r] = stat
        for i, who in enumerate(peers):
            remote(stat_s.at[r], stat_r.at[at + i], ts_sem.at[r], tr_sem.at[r], who).start()
        got = stat_r.at[pl.ds(at, n)]
        everyone = remote(got, got, ts_sem.at[r], tr_sem.at[r], peers[0])
        if r == 2:
            out_grad = node_gradient()
        everyone.wait_recv()
        for i in range(n):
            stat = stat + stat_r[at + i]
        at += n
        stat_copies.append(everyone)

    taken = [
        remote(swap_s.at[c], swap_r.at[c], ws_sem.at[c], wr_sem.at[c], (from_gx, z_hi * 2 + c))
        for c in range(2)
    ]
    for c in range(2):

        @pl.when(jnp.logical_or(from_gx != gx, core != c))
        def _():
            taken[c].wait_recv()

    @pl.when(own_blk == gx)
    def _():
        stay.wait()

    scales = [
        lax.rsqrt(jnp.sum(stat[m : m + 1], axis=-1, keepdims=True) * (1.0 / SIZES[m]) + 1e-06)
        for m in range(4)
    ]
    row = lax.broadcasted_iota(jnp.int32, (16, H), 0) + 14 * (gx * 8 + gy)
    scale = jnp.where(
        row < BOUNDS[0],
        scales[0],
        jnp.where(row < BOUNDS[1], scales[1], jnp.where(row < BOUNDS[2], scales[2], scales[3])),
    )
    left = swap_r[0] * scale
    right = swap_r[1] * scale
    for g in range(2):
        flat[pl.ds(g, 16, stride=4), :] = left[:, g * Q : (g + 1) * Q]
        flat[pl.ds(2 + g, 16, stride=4), :] = right[:, g * Q : (g + 1) * Q]
    wdir[...] = flat[pl.ds(0, 56), :].astype(BF16)

    for q in range(4):

        @pl.when(came[q])
        def _():
            home[q].wait_send()

    for copy in along + stat_copies:
        copy.wait_send()
    for c in range(2):

        @pl.when(jnp.logical_or(own_blk != gx, core != c))
        def _():
            swap[c].wait_send()

    out_node.wait()
    out_edge.wait()
    out_grad.wait()


def hand_over(*refs):
    given, results, held, sem_in, sem_out = refs[:4], refs[4:8], refs[8:12], refs[12], refs[13]
    into = [pltpu.make_async_copy(given[i], held[i], sem_in.at[i]) for i in range(4)]
    out = [pltpu.make_async_copy(held[i], results[i], sem_out.at[i]) for i in range(4)]
    for copy in into:
        copy.start()
    for i in range(4):
        into[i].wait()
        out[i].start()
    for copy in out:
        copy.wait()


def on_device(
    node_latents, edge_latents, edge_w1, edge_b1, edge_w2, node_w1, node_b1, node_w2,
    node_cot, edge_cot, send_count, send_list, tile_recv, tile_send, tile_perm,
):
    hbm = pl.BlockSpec(memory_space=pl.ANY)
    vmem = pl.BlockSpec(memory_space=pltpu.VMEM)
    smem = pl.BlockSpec(memory_space=pltpu.SMEM)
    b = functools.partial(pltpu.VMEM, dtype=BF16)
    f = functools.partial(pltpu.VMEM, dtype=F32)
    sem = lambda n: pltpu.SemaphoreType.DMA((n,))
    scratch = [
        b((2, Q, D)), b((10, Q, D)), b((768, D)), b((3 * D, D)), b((D, D)), b((2 * D, D)), b((D, D)),
        b((H, D)), b((768, D)), b((4, 2, Q, D)), b((6, Q, Q)), b((6, Q, Q)),
        b((D, 768)), b((D, 768)), b((D, H)),
        b((768, D)), b((768, D)), f((768, D)), b((768, D)), f((768, D)), f((768, 1)),
        f((2, Q, D)), f((2, Q, D)), f((2, Q, D)), b((768, D)), b((768, D)), b((768, D)),
        b((H, 2 * D)), b((H, D)), b((H, D)), f((6, Q, D)), b((4, 2, Q, D)), b((4, 2, Q, D)),
        b((H, D)), b((H, D)), b((768, D)),
        b((ROWS, H)), f((ROWS, H)), b((ROWS, H)),
        b((8, 4, BLK, Q)), b((8, 4, BLK, Q)), b((2, 8, BLK, Q)), b((2, 8, BLK, Q)), b((8, BLK, Q)), b((8, BLK, Q)),
        b((4, 2, BLK, Q)), b((4, 2, BLK, Q)), b((3, 2, BLK, Q)), b((3, 2, BLK, Q)),
        f((2, Q, H)), b((8, 32, H)), b((7, 32, H)), f((32, H)), f((2, 16, H)), f((2, 16, H)),
        f((3, 8, Q)), f((23, 8, Q)), f((64, Q)),
        sem(9), sem(3), sem(4), sem(4), sem(4), sem(4), sem(5), sem(5),
        sem(6), sem(6), sem(6), sem(6), sem(6), sem(6), sem(6), sem(6), sem(3), sem(3), sem(3), sem(3),
        sem(7), sem(7), sem(2), sem(2), sem(3), sem(3),
    ]
    shapes = (
        jax.ShapeDtypeStruct((H, D), BF16),
        jax.ShapeDtypeStruct((H, D), BF16),
        jax.ShapeDtypeStruct((768, D), BF16),
        jax.ShapeDtypeStruct((56, Q), BF16),
    )
    results = pl.pallas_call(
        kernel,
        out_shape=shapes,
        in_specs=[smem] * 4 + [vmem] * 3 + [hbm] * 8,
        out_specs=(hbm, hbm, hbm, vmem),
        scratch_shapes=scratch,
        compiler_params=pltpu.CompilerParams(
            collective_id=0, has_side_effects=True, vmem_limit_bytes=56 * 1024 * 1024
        ),
        name="layer",
    )(
        send_count, jnp.transpose(send_list, (0, 1, 3, 2)), tile_recv, tile_send,
        jnp.transpose(tile_perm, (0, 2, 1, 3)),
        edge_b1.reshape(1, D), node_b1.reshape(1, D),
        node_latents.reshape(2, Q, D), edge_latents.reshape(768, D),
        edge_w1, edge_w2, node_w1, node_w2,
        node_cot.reshape(H, D), edge_cot.reshape(768, D),
    )
    nout, ngrad, egrad, wdir = pl.pallas_call(
        hand_over,
        out_shape=shapes,
        in_specs=[hbm] * 4,
        out_specs=(hbm,) * 4,
        scratch_shapes=[b((H, D)), b((H, D)), b((768, D)), b((56, Q)), sem(4), sem(4)],
        name="hand_over",
    )(*results)
    return (
        nout.reshape(1, 1, H, D),
        ngrad.reshape(1, 1, H, D),
        egrad.reshape(1, 1, 768, D),
        wdir.reshape(7168),
    )


def solution(mesh):
    cells = P("gx", "gy", None, None)
    flat = P("gx", "gy", None)
    return jax.shard_map(
        on_device,
        mesh=mesh,
        in_specs=(
            cells, cells, P(), P(), P(), P(), P(), P(), cells, cells,
            flat, cells, flat, flat, cells,
        ),
        out_specs=(cells, cells, cells, P(("gx", "gy"))),
        check_vma=False,
    )
```
